256 devices in a mesh: engine: 32 (over x, y, core), tp: 8 (over z).
Axes of the slice: x: 4, y: 4, z: 8, core: 2. Of those that a mesh axis runs over, the one named last changes fastest.
Arguments:
- outgoing: bfloat16 [384, 32, 4096], P('engine'), may hold values from -24 to 24
- span_target: int32 [32, 12], replicated, may hold values from 0 to 31, as said below
- span_row: int32 [32, 12], replicated, may hold values from 0 to 7
- span_block: int32 [32, 12], replicated, may hold values from 0 to 63
- span_tokens: int32 [32, 12], replicated, may hold values from 1 to 32
- norm_gain: float32 [4096], replicated, may hold values from 0.3 to 3
- key_weight: bfloat16 [4096, 4096], P(None, 'tp'), may hold values from -0.09375 to 0.09375
- value_weight: bfloat16 [4096, 4096], P(None, 'tp'), may hold values from -0.09375 to 0.09375
- fresh_states: bfloat16 [2, 256, 4096], P(None, ('engine', 'tp')), may hold values from -24 to 24
- queries: bfloat16 [2, 256, 4096], P(None, 'engine', 'tp'), may hold values from -16 to 16
- res_keys: bfloat16 [256, 64, 4096], P('engine', None, 'tp'), may hold values from -16 to 16
- res_values: bfloat16 [256, 64, 4096], P('engine', None, 'tp'), may hold values from -6 to 6
- res_len: int32 [256], P('engine'), may hold values from 2 to 64
Outputs:
- attended: bfloat16 [2, 256, 4096], P(None, 'engine', 'tp')
The draws below stay inside these ranges and needn't reach their ends.
Inputs may be any that keep to these rules, and one draw needn't show every extreme that they name: `span_target`: each engine sends its 12 spans to 12 different engines, never to itself; an engine receives at most 24 spans, and some engine receives exactly 24.
All inputs are finite; a program needn't handle non-finite values.
Results may differ from the reference program's by a relative error of at most 0.0071.
Values may be sent and summed in bfloat16 or wider, within the bound.
A program may use at most 64 MiB of HBM per device.

```python
import math
import jax
import jax.numpy as jnp
from jax import lax

D = 4096
HEADS = 32
HD = 128
SPAN = 32
CTX = 2048
STEPS = 2
ROWS = 8
RES = 64
SEND = 12
N_ENGINE = 32


def spread_factors(key, count, low, high):
    return jnp.exp(jax.random.uniform(key, (count,), jnp.float32, math.log(low), math.log(high)))


def draw_outgoing(key, part):
    key = jax.random.fold_in(key, 1)
    base_key, column_key, row_key = jax.random.split(key, 3)
    count = N_ENGINE * SEND
    columns = spread_factors(column_key, D, 0.3, 3.0)
    row_scale = spread_factors(row_key, count * SPAN, 0.5, 2.0).reshape(count, SPAN, 1)
    states = jax.random.normal(base_key, (count, SPAN, D), jnp.float32) * columns * row_scale
    return jnp.clip(states, -24.0, 24.0).astype(jnp.bfloat16)


def draw_fresh_states(key, part):
    key = jax.random.fold_in(key, 2)
    base_key, column_key, row_key = jax.random.split(key, 3)
    count = N_ENGINE * ROWS
    columns = spread_factors(column_key, D, 0.3, 3.0)
    row_scale = spread_factors(row_key, STEPS * count, 0.5, 2.0).reshape(STEPS, count, 1)
    states = jax.random.normal(base_key, (STEPS, count, D), jnp.float32) * columns * row_scale
    return jnp.clip(states, -24.0, 24.0).astype(jnp.bfloat16)


def draw_queries(key, part):
    key = jax.random.fold_in(key, 3)
    queries = jax.random.normal(key, (STEPS, N_ENGINE * ROWS, HEADS * HD), jnp.float32)
    return jnp.clip(queries, -16.0, 16.0).astype(jnp.bfloat16)


def draw_res_keys(key, part):
    key = jax.random.fold_in(key, 4)
    cached = jax.random.normal(key, (N_ENGINE * ROWS, RES, HEADS * HD), jnp.float32)
    return jnp.clip(cached, -16.0, 16.0).astype(jnp.bfloat16)


def draw_span_target(key, part):
    key = jax.random.fold_in(key, 11)
    order_key, hot_key, pick_key = jax.random.split(key, 3)
    offsets = jax.random.permutation(order_key, N_ENGINE - 1)[:2 * SEND] + 1
    first_offsets = offsets[:SEND]
    second_offsets = offsets[SEND:]
    hot_engine = jax.random.randint(hot_key, (), 0, N_ENGINE)
    picks = jax.random.randint(pick_key, (N_ENGINE, SEND), 0, 2)
    column = jnp.arange(SEND)
    picks = picks.at[(hot_engine - first_offsets) % N_ENGINE, column].set(0)
    picks = picks.at[(hot_engine - second_offsets) % N_ENGINE, column].set(1)
    sources = jnp.arange(N_ENGINE)[:, None]
    chosen_offsets = jnp.where(picks == 1, second_offsets[None, :], first_offsets[None, :])
    return ((sources + chosen_offsets) % N_ENGINE).astype(jnp.int32)


def plant(values, key, least, top_value):
    spot = [jax.random.randint(jax.random.fold_in(key, axis), (), 0, length) for axis, length in enumerate(values.shape)]
    widest = values.shape.index(max(values.shape))
    neighbour = spot[:widest] + [(spot[widest] + 1) % values.shape[widest]] + spot[widest + 1:]
    return values.at[tuple(spot)].set(least).at[tuple(neighbour)].set(top_value)


def steps_of(own_key, shape, cuts, least, top_value):
    level = 1.0
    for dim, parts in cuts:
        steps = jax.random.uniform(jax.random.fold_in(jax.random.fold_in(own_key, 6), dim), (parts,), jnp.float32, least / len(cuts), top_value / len(cuts))
        level = level * jnp.repeat(jnp.exp(steps), shape[dim] // parts).reshape((-1,) + (1,) * (len(shape) - 1 - dim))
    return level


def centred(rng, extent, deviation, most, pieces=(), kind=jnp.bfloat16):
    values = deviation * jax.random.normal(rng, extent, jnp.float32)
    if pieces:
        values = values * steps_of(rng, extent, pieces, -0.22, 0.18)
    return jnp.clip(values, -most, most).astype(kind)


def setup_inputs(seed: int = 0) -> dict:
    splits = jax.random.split(jax.random.key(seed), 14)
    return {
        "outgoing": draw_outgoing(jax.random.fold_in(splits[13], 71), 0),
        "span_target": draw_span_target(jax.random.fold_in(splits[13], 71), 0),
        "span_row": plant(jax.random.randint(splits[2], (N_ENGINE, SEND), 0, ROWS), jax.random.fold_in(splits[2], 1), 0, ROWS - 1).astype(jnp.int32),
        "span_block": plant(jax.random.randint(splits[3], (N_ENGINE, SEND), 0, CTX // SPAN), jax.random.fold_in(splits[3], 1), 0, (CTX // SPAN) - 1).astype(jnp.int32),
        "span_tokens": plant(jax.random.randint(splits[4], (N_ENGINE, SEND), 1, SPAN + 1), jax.random.fold_in(splits[4], 1), 1, SPAN).astype(jnp.int32),
        "norm_gain": jnp.clip(jnp.exp(jax.random.uniform(splits[5], (D,), jnp.float32, math.log(0.3), math.log(3.0))), 0.3, 3.0),
        "key_weight": centred(splits[6], (D, HEADS * HD), D ** -0.5, 0.09375, ((1, 8),)),
        "value_weight": centred(splits[7], (D, HEADS * HD), D ** -0.5, 0.09375, ((1, 8),)),
        "fresh_states": draw_fresh_states(jax.random.fold_in(splits[13], 71), 0),
        "queries": draw_queries(jax.random.fold_in(splits[13], 71), 0),
        "res_keys": draw_res_keys(jax.random.fold_in(splits[13], 71), 0),
        "res_values": centred(splits[11], (N_ENGINE * ROWS, RES, HEADS * HD), 1.0, 6.0, ((0, 32), (2, 8))),
        "res_len": plant(jax.random.randint(splits[12], (N_ENGINE * ROWS,), 2, RES + 1), jax.random.fold_in(splits[12], 1), 2, RES).astype(jnp.int32),
    }


rope_base = 1000000.0
norm_eps = 1e-06

def rotate(projected, positions):
    count, full_width = projected.shape
    half_size = HD // 2
    per_head = projected.reshape(count, full_width // HD, HD)
    frequency = jnp.exp(jnp.arange(half_size, dtype=jnp.float32) * (-2.0 * math.log(rope_base) / HD))
    angles = positions.astype(jnp.float32)[:, None] * frequency[None, :]
    cosine_table = jnp.cos(angles)[:, None, :]
    sine_table = jnp.sin(angles)[:, None, :]
    lower_half = per_head[..., :half_size]
    upper_half = per_head[..., half_size:]
    turned = jnp.concatenate([lower_half * cosine_table - upper_half * sine_table, upper_half * cosine_table + lower_half * sine_table], axis=-1)
    return turned.reshape(count, full_width)

def normalize(states, norm_gain):
    widened = states.astype(jnp.float32)
    factor = lax.rsqrt(lax.optimization_barrier(jnp.mean(widened * widened, axis=-1, keepdims=True)) + norm_eps)
    return (widened * factor * norm_gain).astype(jnp.bfloat16)

def project(normed, key_weight, value_weight, positions):
    key_raw = jnp.dot(normed, key_weight, preferred_element_type=jnp.float32)
    values_out = jnp.dot(normed, value_weight, preferred_element_type=jnp.float32).astype(jnp.bfloat16)
    return (rotate(key_raw, positions).astype(jnp.bfloat16), values_out)

def attend(queries, res_keys, res_values, res_len, slot_keys, slot_values, slot_row, slot_tokens, fresh_keys, fresh_values):
    step_count, row_count, full_width = queries.shape
    head_count = full_width // HD
    slot_count, slot_size = (slot_keys.shape[0], slot_keys.shape[1])
    resident = res_keys.shape[1]
    turned = queries.astype(jnp.float32).reshape(step_count, row_count, head_count, HD)
    near_keys = res_keys.astype(jnp.float32).reshape(row_count, resident, head_count, HD)
    moved_keys = slot_keys.astype(jnp.float32).reshape(slot_count * slot_size, head_count, HD)
    newest_keys = fresh_keys.astype(jnp.float32).reshape(step_count, row_count, head_count, HD)
    score_near = jnp.einsum('srhd,rjhd->srhj', turned, near_keys)
    score_moved = jnp.einsum('srhd,khd->srhk', turned, moved_keys)
    score_newest = jnp.einsum('srhd,urhd->srhu', turned, newest_keys)
    live_near = jnp.arange(resident, dtype=jnp.int32)[None, :] < res_len[:, None]
    row_match = slot_row[None, :, None] == jnp.arange(row_count, dtype=jnp.int32)[:, None, None]
    token_live = jnp.arange(slot_size, dtype=jnp.int32)[None, None, :] < slot_tokens[None, :, None]
    live_moved = (row_match & token_live).reshape(row_count, slot_count * slot_size)
    live_newest = jnp.arange(step_count)[None, :] <= jnp.arange(step_count)[:, None]
    scores = jnp.concatenate([jnp.where(live_near[None, :, None, :], score_near, -jnp.inf), jnp.where(live_moved[None, :, None, :], score_moved, -jnp.inf), jnp.where(live_newest[:, None, None, :], score_newest, -jnp.inf)], axis=-1) * (1.0 / math.sqrt(HD))
    row_peak = lax.optimization_barrier(jnp.max(scores, axis=-1, keepdims=True))
    expo = jnp.exp(scores - row_peak)
    weights = (expo / lax.optimization_barrier(jnp.sum(expo, axis=-1, keepdims=True))).astype(jnp.bfloat16).astype(jnp.float32)
    moved_count = slot_count * slot_size
    w_near = weights[..., :resident]
    w_moved = weights[..., resident:resident + moved_count]
    w_newest = weights[..., resident + moved_count:]
    result = jnp.einsum('srhj,rjhd->srhd', w_near, res_values.astype(jnp.float32).reshape(row_count, resident, head_count, HD))
    result = result + jnp.einsum('srhk,khd->srhd', w_moved, slot_values.astype(jnp.float32).reshape(moved_count, head_count, HD))
    result = result + jnp.einsum('srhu,urhd->srhd', w_newest, fresh_values.astype(jnp.float32).reshape(step_count, row_count, head_count, HD))
    return result.reshape(step_count, row_count, full_width).astype(jnp.bfloat16)

def reference(outgoing, span_target, span_row, span_block, span_tokens, norm_gain, key_weight, value_weight, fresh_states, queries, res_keys, res_values, res_len):
    offsets = jnp.arange(SPAN, dtype=jnp.int32)

    def rebuild_one(entry):
        states, block_index = entry
        positions = block_index * SPAN + offsets
        return project(normalize(states, norm_gain), key_weight, value_weight, positions)
    moved_keys, moved_values = lax.map(rebuild_one, (outgoing, span_block.reshape(-1).astype(jnp.int32)))
    flat_target = span_target.reshape(-1)
    flat_row = span_row.reshape(-1)
    flat_tokens = span_tokens.reshape(-1)
    fresh_positions = CTX + jnp.repeat(jnp.arange(STEPS, dtype=jnp.int32), ROWS)

    def one_engine(engine):
        first_row = (engine * ROWS).astype(jnp.int32)
        query_part = lax.dynamic_slice_in_dim(queries, first_row, ROWS, 1)
        fresh_part = lax.dynamic_slice_in_dim(fresh_states, first_row, ROWS, 1)
        near_keys = lax.dynamic_slice_in_dim(res_keys, first_row, ROWS, 0)
        near_values = lax.dynamic_slice_in_dim(res_values, first_row, ROWS, 0)
        near_len = lax.dynamic_slice_in_dim(res_len, first_row, ROWS, 0)
        new_keys, new_values = project(normalize(fresh_part.reshape(STEPS * ROWS, D), norm_gain), key_weight, value_weight, fresh_positions)
        slot_row = jnp.where(flat_target == engine, flat_row, -1)
        return attend(query_part, near_keys, near_values, near_len, moved_keys, moved_values, slot_row, flat_tokens, new_keys.reshape(STEPS, ROWS, -1), new_values.reshape(STEPS, ROWS, -1))
    per_engine = lax.map(one_engine, jnp.arange(N_ENGINE, dtype=jnp.int32))
    return per_engine.transpose(1, 0, 2, 3).reshape(STEPS, N_ENGINE * ROWS, HEADS * HD)
```

```python
import functools
import math

import jax
import jax.numpy as jnp
import numpy as np
from jax import lax
from jax.experimental import pallas as pl
from jax.experimental.pallas import tpu as pltpu
from jax.sharding import PartitionSpec as P

MESH = pl.DeviceIdType.MESH
F32 = jnp.float32
BF16 = jnp.bfloat16
HD = 128
HALF = HD // 2
CTX = 2048
SPAN = 32
ROPE_BASE = 1000000.0
NORM_EPS = 1e-06
NEG = -1e30


def iota(shape, axis):
    return lax.broadcasted_iota(jnp.int32, shape, axis)


def rope_tables(steps):
    frequency = ROPE_BASE ** (-2.0 * np.arange(HALF) / HD)
    blocks = np.arange(CTX // SPAN + 8)[:, None] * SPAN * frequency[None, :]
    tokens = np.arange(SPAN)[:, None] * frequency[None, :]

    def wide(angles):
        cosine, sine = np.cos(angles), np.sin(angles)
        return np.concatenate([cosine, cosine], 1), np.concatenate([-sine, sine], 1)

    return np.concatenate([*wide(blocks), *wide(tokens)], 0).astype(np.float32)


def dot(a, b):
    return jnp.dot(a, b, preferred_element_type=F32)


def dot_nt(a, b):
    return lax.dot_general(a, b, (((1,), (1,)), ((), ())), preferred_element_type=F32)


def per_head(x, count):
    return [x[:, h * HD : (h + 1) * HD] for h in range(count)]


def own_head(x, heads, head_of_row):
    blocks = per_head(x, heads)
    out = blocks[0]
    for h in range(1, heads):
        out = jnp.where(head_of_row == h, blocks[h], out)
    return out


def spread_heads(x, heads, head_of_row):
    return jnp.concatenate(
        [jnp.where(head_of_row == h, x, 0.0) for h in range(heads)], axis=1
    )


def kernel(
    engines,
    tps,
    sends,
    rows,
    steps,
    x_hbm,
    tgt_s,
    blk_s,
    tok_s,
    len_s,
    tgt_v,
    row_v,
    gain_v,
    tab_v,
    fresh_v,
    q_v,
    wk_hbm,
    wv_hbm,
    rk_hbm,
    rv_hbm,
    out_v,
    xv,
    nv,
    wk,
    wv,
    rk,
    rv,
    kb,
    vb,
    cosv,
    sinv,
    fst32,
    fst,
    fin,
    qob,
    qib,
    pob,
    pib,
    sem_x,
    sem_w,
    sem_r,
    sem_f,
    sem_q,
    sem_p,
):
    me = lax.axis_index("engine")
    z = lax.axis_index("tp")
    width = wk.shape[1]
    depth = wk.shape[0]
    heads = width // HD
    sh = steps * heads
    pairs = engines * sh
    inner = sh * rows
    tokens = sends * SPAN
    x_parts = sem_x.shape[0]
    x_rows = tokens // x_parts
    w_parts = sem_w.shape[1]
    w_cols = width // w_parts

    def x_copy(i):
        part = pl.ds(i * x_rows, x_rows)
        return pltpu.make_async_copy(x_hbm.at[part], xv.at[part], sem_x.at[i])

    def w_copy(m, i):
        part = pl.ds(i * w_cols, w_cols)
        source, target = ((wk_hbm, wk), (wv_hbm, wv))[m]
        return pltpu.make_async_copy(source.at[:, part], target.at[:, part], sem_w.at[m, i])

    for i in range(x_parts):
        x_copy(i).start()
    for m in range(2):
        for i in range(w_parts):
            w_copy(m, i).start()
    rk_copy = pltpu.make_async_copy(rk_hbm, rk, sem_r.at[0])
    rv_copy = pltpu.make_async_copy(rv_hbm, rv, sem_r.at[1])
    rk_copy.start()
    rv_copy.start()

    barrier = pltpu.get_barrier_semaphore()

    def greet_engine(i, carry):
        other = lax.rem(me + i, engines)
        pl.semaphore_signal(barrier, inc=1, device_id=(other, z), device_id_type=MESH)
        return carry

    def greet_tp(i, carry):
        other = lax.rem(z + i, tps)
        pl.semaphore_signal(barrier, inc=1, device_id=(me, other), device_id_type=MESH)
        return carry

    lax.fori_loop(1, engines, greet_engine, 0)
    lax.fori_loop(1, tps, greet_tp, 0)

    gain = gain_v[...]
    fw = depth // 8
    fresh = fresh_v[...].astype(F32)
    fresh = fresh * lax.rsqrt(jnp.mean(fresh * fresh, axis=1, keepdims=True) + NORM_EPS) * gain
    for s in range(steps):
        for c in range(8):
            fst32[s * 8 + c : s * 8 + c + 1, :] = fresh[s : s + 1, c * fw : (c + 1) * fw]
    fst[...] = fst32[...].astype(BF16)
    fin[z] = fst[...]

    q = q_v[...].astype(F32)
    q64 = jnp.concatenate(
        [q[s][:, h * HD : (h + 1) * HD] for s in range(steps) for h in range(heads)], axis=0
    )
    hit = tgt_v[...] == me
    arrives = jnp.sum(jnp.where(hit, (row_v[...] + 1).astype(F32), 0.0), axis=0, keepdims=True)
    pe = iota((pairs, engines), 0) // sh
    row_col = jnp.sum(
        jnp.where(pe == iota((pairs, engines), 1), arrives, 0.0), axis=1, keepdims=True
    )
    arr_col = jnp.sum(
        jnp.where(
            iota((engines, engines), 0) == iota((engines, engines), 1), arrives, 0.0
        ),
        axis=1,
        keepdims=True,
    )
    row_lane = jnp.sum(
        jnp.where(
            iota((engines, pairs), 0) == iota((engines, pairs), 1) // sh, arr_col, 0.0
        ),
        axis=0,
        keepdims=True,
    )
    gi, gl = iota((pairs, inner), 0), iota((pairs, inner), 1)
    pick = (row_col == (gl % rows + 1).astype(F32)) & (gi % sh == gl // rows)
    ti, tl = iota((inner, pairs), 0), iota((inner, pairs), 1)
    pick_t = (row_lane == (ti % rows + 1).astype(F32)) & (tl % sh == ti // rows)
    qout = dot(jnp.where(pick, 1.0, 0.0).astype(BF16), q64.astype(BF16))
    qob[...] = qout.reshape(engines, sh, HD)
    qib[me] = jnp.zeros((sh, HD), F32)

    pl.semaphore_wait(barrier, engines - 1 + tps - 1)

    def q_copy(i):
        other = lax.rem(me + i, engines)
        return pltpu.make_async_remote_copy(
            src_ref=qob.at[other],
            dst_ref=qib.at[me],
            send_sem=sem_q.at[0],
            recv_sem=sem_q.at[1],
            device_id=(other, z),
            device_id_type=MESH,
        )

    def f_copy(i):
        other = lax.rem(z + i, tps)
        return pltpu.make_async_remote_copy(
            src_ref=fst,
            dst_ref=fin.at[z],
            send_sem=sem_f.at[0],
            recv_sem=sem_f.at[1],
            device_id=(me, other),
            device_id_type=MESH,
        )

    def start_q(i, carry):
        q_copy(i).start()
        return carry

    def start_f(i, carry):
        f_copy(i).start()
        return carry

    lax.fori_loop(1, engines, start_q, 0)
    lax.fori_loop(1, tps, start_f, 0)

    nb = CTX // SPAN + 8
    tok_cos = tab_v[2 * nb : 2 * nb + SPAN, :]
    tok_sin = tab_v[2 * nb + SPAN : 2 * nb + 2 * SPAN, :]
    lane_token = iota((1, tokens), 1)
    col_target = jnp.full((1, tokens), -1, jnp.int32)
    for k in range(sends):
        b = blk_s[k, me]
        block_cos = tab_v[pl.ds(b, 1), :]
        block_sin = tab_v[pl.ds(b + nb, 1), :]
        cosv[k * SPAN : (k + 1) * SPAN, :] = block_cos * tok_cos - block_sin * tok_sin
        sinv[k * SPAN : (k + 1) * SPAN, :] = block_sin * tok_cos + block_cos * tok_sin
        live = (lane_token >= k * SPAN) & (lane_token < k * SPAN + tok_s[k, me])
        col_target = jnp.where(live, tgt_s[k, me], col_target)

    for i in range(x_parts):
        x_copy(i).wait()

        def norm_step(j, carry, i=i):
            part = pl.ds(pl.multiple_of(i * x_rows + j * 16, 16), 16)
            block = xv[part, :].astype(F32)
            factor = lax.rsqrt(jnp.mean(block * block, axis=1, keepdims=True) + NORM_EPS)
            nv[part, :] = (block * factor * gain).astype(BF16)
            return carry

        lax.fori_loop(0, x_rows // 16, norm_step, 0)

    def turn(raw, cosine, sine):
        return raw * cosine + pltpu.roll(raw, HALF, 1) * sine

    for i in range(w_parts):
        w_copy(0, i).wait()
        raw = dot(nv[...], wk[:, i * w_cols : (i + 1) * w_cols])
        for h in range(w_cols // HD):
            turned = turn(raw[:, h * HD : (h + 1) * HD], cosv[...], sinv[...])
            kb[:, i * w_cols + h * HD : i * w_cols + (h + 1) * HD] = turned.astype(BF16)
    for i in range(w_parts):
        w_copy(1, i).wait()
        vb[:, i * w_cols : (i + 1) * w_cols] = dot(
            nv[...], wv[:, i * w_cols : (i + 1) * w_cols]
        ).astype(BF16)

    scale = 1.0 / math.sqrt(HD)
    everyone = pltpu.make_async_remote_copy(
        src_ref=qob.at[pl.ds(0, engines - 1)],
        dst_ref=qib.at[pl.ds(0, engines - 1)],
        send_sem=sem_q.at[0],
        recv_sem=sem_q.at[1],
        device_id=(me, z),
        device_id_type=MESH,
    )
    everyone.wait_recv()
    pair_row = iota((pairs, 1), 0)
    pair_head = pair_row % heads
    qin = qib[...].reshape(pairs, HD)
    s = dot_nt(spread_heads(qin, heads, pair_head).astype(BF16), kb[...]) * scale
    live = col_target == pair_row // sh
    s = jnp.where(live, s, NEG)
    peak = jnp.max(s, axis=1, keepdims=True)
    p = jnp.where(live, jnp.exp(s - peak), 0.0)
    total = jnp.maximum(jnp.sum(p, axis=1, keepdims=True), 1e-30)
    o = own_head(dot(p.astype(BF16), vb[...]), heads, pair_head) / total
    lse = peak + jnp.log(total)
    hi = lse.astype(BF16).astype(F32)
    mid = (lse - hi).astype(BF16).astype(F32)
    low = lse - hi - mid
    lane = iota((pairs, HD), 1)
    coded = jnp.where(lane < 32, hi, jnp.where(lane < 64, mid, low))
    pob[...] = jnp.concatenate(
        [o.reshape(engines, sh, HD), coded.reshape(engines, sh, HD)], axis=1
    ).astype(BF16)

    def p_copy(i):
        other = lax.rem(me + i, engines)
        return pltpu.make_async_remote_copy(
            src_ref=pob.at[other],
            dst_ref=pib.at[me],
            send_sem=sem_p.at[0],
            recv_sem=sem_p.at[1],
            device_id=(other, z),
            device_id_type=MESH,
        )

    def start_p(i, carry):
        p_copy(i).start()
        return carry

    lax.fori_loop(1, engines, start_p, 0)
    pib[me] = jnp.zeros((2 * sh, HD), BF16)

    fresh_all = pltpu.make_async_remote_copy(
        src_ref=fin.at[pl.ds(0, tps - 1)],
        dst_ref=fin.at[pl.ds(0, tps - 1)],
        send_sem=sem_f.at[0],
        recv_sem=sem_f.at[1],
        device_id=(me, z),
        device_id_type=MESH,
    )
    fresh_all.wait_recv()
    fr = rows * steps * 8
    ri, rl = iota((fr, fr), 0), iota((fr, fr), 1)
    want = (ri % rows) * (steps * 8) + (ri // rows % steps) * 8 + ri // (rows * steps)
    order = jnp.where(rl == want, 1.0, 0.0).astype(BF16)
    sorted_fresh = dot(order, fin[...].reshape(fr, fw)).astype(BF16)
    new = rows * steps
    fn = jnp.concatenate(
        [sorted_fresh[c * new : (c + 1) * new, :] for c in range(8)], axis=1
    )
    f_step = iota((new, 1), 0) // rows
    f_cos = jnp.zeros((new, HD), F32)
    f_sin = jnp.zeros((new, HD), F32)
    bc = CTX // SPAN
    for t in range(steps):
        c0, s0 = tab_v[bc : bc + 1, :], tab_v[nb + bc : nb + bc + 1, :]
        c1, s1 = tok_cos[t : t + 1, :], tok_sin[t : t + 1, :]
        f_cos = jnp.where(f_step == t, c0 * c1 - s0 * s1, f_cos)
        f_sin = jnp.where(f_step == t, s0 * c1 + c0 * s1, f_sin)
    raw = dot(fn, wk[...])
    fk = jnp.concatenate([turn(b, f_cos, f_sin) for b in per_head(raw, heads)], axis=1).astype(BF16)
    fv = dot(fn, wv[...]).astype(BF16)

    near = rk.shape[0]
    resident = near // rows
    rk_copy.wait()
    rv_copy.wait()
    in_row = iota((inner, 1), 0)
    in_head = in_row // rows % heads
    q_near = spread_heads(q64, heads, in_head).astype(BF16)
    lane_near = iota((1, near), 1)
    col_row = jnp.full((1, near), -1, jnp.int32)
    for r in range(rows):
        ok = (lane_near >= r * resident) & (lane_near < r * resident + len_s[r])
        col_row = jnp.where(ok, r, col_row)
    live_near = col_row == in_row % rows
    lane_new = iota((1, new), 1)
    live_new = (lane_new % rows == in_row % rows) & (lane_new // rows <= in_row // (rows * heads))
    s_near = jnp.where(live_near, dot_nt(q_near, rk[...]) * scale, NEG)
    s_new = jnp.where(live_new, dot_nt(q_near, fk) * scale, NEG)
    peak_n = jnp.maximum(
        jnp.max(s_near, axis=1, keepdims=True), jnp.max(s_new, axis=1, keepdims=True)
    )
    p_near = jnp.where(live_near, jnp.exp(s_near - peak_n), 0.0)
    p_new = jnp.where(live_new, jnp.exp(s_new - peak_n), 0.0)
    total_n = jnp.sum(p_near, axis=1, keepdims=True) + jnp.sum(p_new, axis=1, keepdims=True)
    o_near = own_head(
        dot(p_near.astype(BF16), rv[...]) + dot(p_new.astype(BF16), fv), heads, in_head
    )

    from_all = pltpu.make_async_remote_copy(
        src_ref=pob.at[pl.ds(0, engines - 1)],
        dst_ref=pib.at[pl.ds(0, engines - 1)],
        send_sem=sem_p.at[0],
        recv_sem=sem_p.at[1],
        device_id=(me, z),
        device_id_type=MESH,
    )
    from_all.wait_recv()
    pin = pib[...].astype(F32)
    o_in = pin[:, :sh, :].reshape(pairs, HD)
    parts = pin[:, sh:, :].reshape(pairs, HD)
    lse_in = parts[:, 0:1] + parts[:, 32:33] + parts[:, 64:65]
    eye = iota((inner, inner), 0) == iota((inner, inner), 1)
    peak_lane = jnp.sum(jnp.where(eye, peak_n, 0.0), axis=0, keepdims=True)
    top = jnp.maximum(
        jnp.max(jnp.where(pick, lse_in, NEG), axis=0, keepdims=True), peak_lane
    )
    top_pair = jnp.sum(jnp.where(pick, top, 0.0), axis=1, keepdims=True)
    top_in = jnp.sum(jnp.where(eye, top, 0.0), axis=1, keepdims=True)
    valid = row_col > 0.0
    w_in = jnp.where(valid, jnp.exp(jnp.where(valid, lse_in - top_pair, 0.0)), 0.0)
    weighted = jnp.concatenate(
        [jnp.where(valid, w_in * o_in, 0.0), jnp.broadcast_to(w_in, (pairs, HD))], axis=1
    )
    first = weighted.astype(BF16)
    second = (weighted - first.astype(F32)).astype(BF16)
    collect = jnp.where(pick_t, 1.0, 0.0).astype(BF16)
    gathered = dot(collect, first) + dot(collect, second)
    w_near = jnp.exp(peak_n - top_in)
    result = (w_near * o_near + gathered[:, :HD]) / (w_near * total_n + gathered[:, HD:])
    for t in range(steps):
        for h in range(heads):
            j = t * heads + h
            out_v[t, :, h * HD : (h + 1) * HD] = result[j * rows : (j + 1) * rows, :].astype(BF16)

    everyone.wait_send()
    fresh_all.wait_send()
    from_all.wait_send()


def per_device(
    engines,
    tps,
    outgoing,
    span_target,
    span_row,
    span_block,
    span_tokens,
    norm_gain,
    key_weight,
    value_weight,
    fresh_states,
    queries,
    res_keys,
    res_values,
    res_len,
):
    sends, span, depth = outgoing.shape
    width = key_weight.shape[1]
    steps, rows, _ = queries.shape
    resident = res_keys.shape[1]
    heads = width // HD
    sh = steps * heads
    tokens = sends * span
    vmem = pl.BlockSpec(memory_space=pltpu.VMEM)
    smem = pl.BlockSpec(memory_space=pltpu.SMEM)
    hbm = pl.BlockSpec(memory_space=pltpu.HBM)
    target_t = span_target.T
    x_parts, w_parts = 3, 2
    return pl.pallas_call(
        functools.partial(kernel, engines, tps, sends, rows, steps),
        out_shape=jax.ShapeDtypeStruct((steps, rows, width), BF16),
        in_specs=[hbm, smem, smem, smem, smem, vmem, vmem, vmem, vmem, vmem, vmem, hbm, hbm, hbm, hbm],
        out_specs=vmem,
        scratch_shapes=[
            pltpu.VMEM((tokens, depth), BF16),
            pltpu.VMEM((tokens, depth), BF16),
            pltpu.VMEM((depth, width), BF16),
            pltpu.VMEM((depth, width), BF16),
            pltpu.VMEM((rows * resident, width), BF16),
            pltpu.VMEM((rows * resident, width), BF16),
            pltpu.VMEM((tokens, width), BF16),
            pltpu.VMEM((tokens, width), BF16),
            pltpu.VMEM((tokens, HD), F32),
            pltpu.VMEM((tokens, HD), F32),
            pltpu.VMEM((steps * 8, depth // 8), F32),
            pltpu.VMEM((steps * 8, depth // 8), BF16),
            pltpu.VMEM((tps, steps * 8, depth // 8), BF16),
            pltpu.VMEM((engines, sh, HD), F32),
            pltpu.VMEM((engines, sh, HD), F32),
            pltpu.VMEM((engines, 2 * sh, HD), BF16),
            pltpu.VMEM((engines, 2 * sh, HD), BF16),
            pltpu.SemaphoreType.DMA((x_parts,)),
            pltpu.SemaphoreType.DMA((2, w_parts)),
            pltpu.SemaphoreType.DMA((2,)),
            pltpu.SemaphoreType.DMA((2,)),
            pltpu.SemaphoreType.DMA((2,)),
            pltpu.SemaphoreType.DMA((2,)),
        ],
        compiler_params=pltpu.CompilerParams(
            collective_id=0, has_side_effects=True, vmem_limit_bytes=60 * 1024 * 1024
        ),
    )(
        outgoing.reshape(tokens, depth),
        target_t,
        span_block.T,
        span_tokens.T,
        res_len,
        target_t,
        span_row.T,
        norm_gain.reshape(1, depth),
        jnp.asarray(rope_tables(steps)),
        fresh_states.reshape(steps, depth),
        queries,
        key_weight,
        value_weight,
        res_keys.reshape(rows * resident, width),
        res_values.reshape(rows * resident, width),
    )


def solution(mesh):
    in_specs = (
        P("engine", None, None),
        P(),
        P(),
        P(),
        P(),
        P(),
        P(None, "tp"),
        P(None, "tp"),
        P(None, ("engine", "tp"), None),
        P(None, "engine", "tp"),
        P("engine", None, "tp"),
        P("engine", None, "tp"),
        P("engine"),
    )
    return jax.shard_map(
        functools.partial(per_device, mesh.shape["engine"], mesh.shape["tp"]),
        mesh=mesh,
        in_specs=in_specs,
        out_specs=P(None, "engine", "tp"),
        check_vma=False,
    )
```

```python
import functools
import math

import jax
import jax.numpy as jnp
import numpy as np
from jax import lax
from jax.experimental import pallas as pl
from jax.experimental.pallas import tpu as pltpu
from jax.sharding import PartitionSpec as P

MESH = pl.DeviceIdType.MESH
F32 = jnp.float32
BF16 = jnp.bfloat16
HD = 128
HALF = HD // 2
CTX = 2048
SPAN = 32
ROPE_BASE = 1000000.0
NORM_EPS = 1e-06
NEG = -1e30


def iota(shape, axis):
    return lax.broadcasted_iota(jnp.int32, shape, axis)


def rope_tables(steps):
    frequency = ROPE_BASE ** (-2.0 * np.arange(HALF) / HD)
    blocks = np.arange(CTX // SPAN + 8)[:, None] * SPAN * frequency[None, :]
    tokens = np.arange(SPAN)[:, None] * frequency[None, :]

    def wide(angles):
        cosine, sine = np.cos(angles), np.sin(angles)
        return np.concatenate([cosine, cosine], 1), np.concatenate([-sine, sine], 1)

    return np.concatenate([*wide(blocks), *wide(tokens)], 0).astype(np.float32)


def dot(a, b):
    return jnp.dot(a, b, preferred_element_type=F32)


def dot_nt(a, b):
    return lax.dot_general(a, b, (((1,), (1,)), ((), ())), preferred_element_type=F32)


def per_head(x, count):
    return [x[:, h * HD : (h + 1) * HD] for h in range(count)]


def own_head(x, heads, head_of_row):
    blocks = per_head(x, heads)
    out = blocks[0]
    for h in range(1, heads):
        out = jnp.where(head_of_row == h, blocks[h], out)
    return out


def spread_heads(x, heads, head_of_row):
    return jnp.concatenate(
        [jnp.where(head_of_row == h, x, 0.0) for h in range(heads)], axis=1
    )


def kernel(
    engines,
    tps,
    sends,
    rows,
    steps,
    x_hbm,
    tgt_hbm,
    row_hbm,
    blk_hbm,
    tok_hbm,
    len_hbm,
    gain_hbm,
    tab_hbm,
    fresh_hbm,
    q_hbm,
    wk_hbm,
    wv_hbm,
    rk_hbm,
    rv_hbm,
    out_v,
    xv,
    nv,
    wk,
    wv,
    rk,
    rv,
    ak,
    av,
    kb,
    vb,
    squares,
    cosv,
    sinv,
    fst32,
    fst,
    fin,
    qob,
    qib,
    pob,
    pib,
    place,
    tgt_s,
    blk_s,
    tok_s,
    len_s,
    tgt_v,
    row_v,
    gain_v,
    tab_v,
    fresh_v,
    q_v,
    sem_x,
    sem_w,
    sem_r,
    sem_s,
    sem_f,
    sem_q,
    sem_p,
):
    me = lax.axis_index("engine")
    z = lax.axis_index("tp")
    width = wk.shape[1]
    depth = wk.shape[0]
    heads = width // HD
    sh = steps * heads
    pairs = engines * sh
    inner = sh * rows
    tokens = sends * SPAN
    chunks = sem_x.shape[0]
    chunk = depth // chunks

    def x_copy(c):
        part = pl.ds(c * chunk, chunk)
        return pltpu.make_async_copy(x_hbm.at[:, part], xv.at[:, part], sem_x.at[c])

    def w_copy(m, c):
        part = pl.ds(c * chunk, chunk)
        source, target = ((wk_hbm, wk), (wv_hbm, wv))[m]
        return pltpu.make_async_copy(source.at[part], target.at[part], sem_w.at[m, c])

    small = [
        pltpu.make_async_copy(source, target, sem_s.at[i])
        for i, (source, target) in enumerate(
            (
                (gain_hbm, gain_v),
                (fresh_hbm, fresh_v),
                (q_hbm, q_v),
                (tgt_hbm, tgt_v),
                (row_hbm, row_v),
                (tgt_hbm, tgt_s),
                (blk_hbm, blk_s),
                (tok_hbm, tok_s),
                (tab_hbm, tab_v),
                (len_hbm, len_s),
            )
        )
    ]
    x_copy(0).start()
    for copy in small[:5]:
        copy.start()
    for c in range(chunks):
        w_copy(0, c).start()
        w_copy(1, c).start()
        if c + 1 < chunks:
            x_copy(c + 1).start()
        if c == 0:
            for copy in small[5:]:
                copy.start()
    rk_copy = pltpu.make_async_copy(rk_hbm, rk, sem_r.at[0])
    rv_copy = pltpu.make_async_copy(rv_hbm, rv, sem_r.at[1])
    rk_copy.start()
    rv_copy.start()

    barrier = pltpu.get_barrier_semaphore()

    def greet_engine(i, carry):
        other = lax.rem(me + i, engines)
        pl.semaphore_signal(barrier, inc=1, device_id=(other, z), device_id_type=MESH)
        return carry

    def greet_tp(i, carry):
        other = lax.rem(z + i, tps)
        pl.semaphore_signal(barrier, inc=1, device_id=(me, other), device_id_type=MESH)
        return carry

    lax.fori_loop(1, engines, greet_engine, 0)
    lax.fori_loop(1, tps, greet_tp, 0)

    small[0].wait()
    small[1].wait()
    fw = depth // 8
    fresh = fresh_v[...].astype(F32)
    fresh = fresh * lax.rsqrt(jnp.mean(fresh * fresh, axis=1, keepdims=True) + NORM_EPS)
    fresh = fresh * gain_v[...]
    for s in range(steps):
        for c in range(8):
            fst32[s * 8 + c : s * 8 + c + 1, :] = fresh[s : s + 1, c * fw : (c + 1) * fw]
    fst[...] = fst32[...].astype(BF16)
    fin[z] = fst[...]

    for copy in small[2:5]:
        copy.wait()
    q = q_v[...].astype(F32)
    q64 = jnp.concatenate(
        [q[s][:, h * HD : (h + 1) * HD] for s in range(steps) for h in range(heads)], axis=0
    )
    hit = tgt_v[...] == me
    arrives = jnp.sum(jnp.where(hit, (row_v[...] + 1).astype(F32), 0.0), axis=0, keepdims=True)
    pe = iota((pairs, engines), 0) // sh
    row_col = jnp.sum(
        jnp.where(pe == iota((pairs, engines), 1), arrives, 0.0), axis=1, keepdims=True
    )
    arr_col = jnp.sum(
        jnp.where(
            iota((engines, engines), 0) == iota((engines, engines), 1), arrives, 0.0
        ),
        axis=1,
        keepdims=True,
    )
    row_lane = jnp.sum(
        jnp.where(
            iota((engines, pairs), 0) == iota((engines, pairs), 1) // sh, arr_col, 0.0
        ),
        axis=0,
        keepdims=True,
    )
    gi, gl = iota((pairs, inner), 0), iota((pairs, inner), 1)
    pick = (row_col == (gl % rows + 1).astype(F32)) & (gi % sh == gl // rows)
    ti, tl = iota((inner, pairs), 0), iota((inner, pairs), 1)
    pick_t = (row_lane == (ti % rows + 1).astype(F32)) & (tl % sh == ti // rows)
    qout = dot(jnp.where(pick, 1.0, 0.0).astype(BF16), q64.astype(BF16))
    qob[...] = qout.reshape(engines, sh, HD)
    qib[me] = jnp.zeros((sh, HD), F32)

    for copy in small[5:]:
        copy.wait()
    nb = CTX // SPAN + 8
    tok_cos = tab_v[2 * nb : 2 * nb + SPAN, :]
    tok_sin = tab_v[2 * nb + SPAN : 2 * nb + 2 * SPAN, :]
    span_lane = iota((1, sends * sh), 1)
    lane_target = jnp.full((1, sends * sh), -1, jnp.int32)
    for k in range(sends):
        b = blk_s[k, me]
        block_cos = tab_v[pl.ds(b, 1), :]
        block_sin = tab_v[pl.ds(b + nb, 1), :]
        cosv[k * SPAN : (k + 1) * SPAN, :] = block_cos * tok_cos - block_sin * tok_sin
        sinv[k * SPAN : (k + 1) * SPAN, :] = block_sin * tok_cos + block_cos * tok_sin
        lane_target = jnp.where(span_lane // sh == k, tgt_s[k, me], lane_target)
    oi, ol = iota((pairs, sends * sh), 0), iota((pairs, sends * sh), 1)
    place[...] = jnp.where((lane_target == oi // sh) & (oi % sh == ol % sh), 1.0, 0.0).astype(BF16)

    def q_copy(i):
        other = lax.rem(me + i, engines)
        return pltpu.make_async_remote_copy(
            src_ref=qob.at[other],
            dst_ref=qib.at[me],
            send_sem=sem_q.at[0],
            recv_sem=sem_q.at[1],
            device_id=(other, z),
            device_id_type=MESH,
        )

    def f_copy(i):
        other = lax.rem(z + i, tps)
        return pltpu.make_async_remote_copy(
            src_ref=fst,
            dst_ref=fin.at[z],
            send_sem=sem_f.at[0],
            recv_sem=sem_f.at[1],
            device_id=(me, other),
            device_id_type=MESH,
        )

    def start_q(i, carry):
        q_copy(i).start()
        return carry

    def start_f(i, carry):
        f_copy(i).start()
        return carry

    def turn(raw, cosine, sine):
        return raw * cosine + pltpu.roll(raw, HALF, 1) * sine

    for c in range(chunks):
        part = slice(c * chunk, (c + 1) * chunk)
        x_copy(c).wait()
        block = xv[:, part].astype(F32)
        nv[:, part] = (block * gain_v[:, part]).astype(BF16)
        sq = block * block
        folded = sum(sq[:, j * HD : (j + 1) * HD] for j in range(chunk // HD))
        squares[...] = folded if c == 0 else squares[...] + folded
        last = c == chunks - 1
        if last:
            mean = jnp.sum(squares[...], axis=1, keepdims=True) * (1.0 / depth)
            factor = lax.rsqrt(mean + NORM_EPS)
            cosv[...] = cosv[...] * factor
            sinv[...] = sinv[...] * factor
        w_copy(0, c).wait()
        raw = dot(nv[:, part], wk[part, :])
        raw = raw if c == 0 else ak[...] + raw
        if last:
            for h in range(heads):
                head = slice(h * HD, (h + 1) * HD)
                kb[:, head] = turn(raw[:, head], cosv[...], sinv[...]).astype(BF16)
        else:
            ak[...] = raw
        w_copy(1, c).wait()
        raw = dot(nv[:, part], wv[part, :])
        raw = raw if c == 0 else av[...] + raw
        if last:
            vb[...] = (raw * factor).astype(BF16)
        else:
            av[...] = raw
        if c == chunks // 2 - 1:
            pl.semaphore_wait(barrier, engines - 1 + tps - 1)
            lax.fori_loop(1, engines, start_q, 0)
            lax.fori_loop(1, tps, start_f, 0)

    scale = 1.0 / math.sqrt(HD)
    everyone = pltpu.make_async_remote_copy(
        src_ref=qob.at[pl.ds(0, engines - 1)],
        dst_ref=qib.at[pl.ds(0, engines - 1)],
        send_sem=sem_q.at[0],
        recv_sem=sem_q.at[1],
        device_id=(me, z),
        device_id_type=MESH,
    )
    everyone.wait_recv()
    made = []
    for g in range(0, sends, HD // SPAN):
        spans = range(g, min(g + HD // SPAN, sends))
        count = len(spans)
        group = slice(g * SPAN, (g + count) * SPAN)
        q_g = jnp.concatenate([qib[tgt_s[k, me]] for k in spans], axis=0)
        g_row = iota((count * sh, 1), 0)
        g_lane = iota((1, count * SPAN), 1)
        edge = jnp.zeros((count * sh, 1), jnp.int32)
        for j, k in enumerate(spans):
            edge = jnp.where(g_row // sh == j, j * SPAN + tok_s[k, me], edge)
        live = (g_lane >= g_row // sh * SPAN) & (g_lane < edge)
        s = dot_nt(spread_heads(q_g, heads, g_row % heads).astype(BF16), kb[group, :]) * scale
        s = jnp.where(live, s, NEG)
        peak = jnp.max(s, axis=1, keepdims=True)
        p = jnp.where(live, jnp.exp(s - peak), 0.0)
        total = jnp.sum(p, axis=1, keepdims=True)
        o = own_head(dot(p.astype(BF16), vb[group, :]), heads, g_row % heads) / total
        lse = peak + jnp.log(total)
        hi = lse.astype(BF16).astype(F32)
        mid = (lse - hi).astype(BF16).astype(F32)
        low = lse - hi - mid
        lane = iota((count * sh, HD), 1)
        coded = jnp.where(lane < 32, hi, jnp.where(lane < 64, mid, low))
        made.append(jnp.concatenate([o, coded], axis=1).astype(BF16))
    placed = dot(place[...], jnp.concatenate(made, axis=0))
    pob[...] = jnp.concatenate(
        [placed[:, :HD].reshape(engines, sh, HD), placed[:, HD:].reshape(engines, sh, HD)], axis=1
    ).astype(BF16)

    def p_copy(i):
        other = lax.rem(me + i, engines)
        return pltpu.make_async_remote_copy(
            src_ref=pob.at[other],
            dst_ref=pib.at[me],
            send_sem=sem_p.at[0],
            recv_sem=sem_p.at[1],
            device_id=(other, z),
            device_id_type=MESH,
        )

    def start_p(i, carry):
        p_copy(i).start()
        return carry

    lax.fori_loop(1, engines, start_p, 0)
    pib[me] = jnp.zeros((2 * sh, HD), BF16)

    fresh_all = pltpu.make_async_remote_copy(
        src_ref=fin.at[pl.ds(0, tps - 1)],
        dst_ref=fin.at[pl.ds(0, tps - 1)],
        send_sem=sem_f.at[0],
        recv_sem=sem_f.at[1],
        device_id=(me, z),
        device_id_type=MESH,
    )
    fresh_all.wait_recv()
    fr = rows * steps * 8
    ri, rl = iota((fr, fr), 0), iota((fr, fr), 1)
    want = (ri % rows) * (steps * 8) + (ri // rows % steps) * 8 + ri // (rows * steps)
    order = jnp.where(rl == want, 1.0, 0.0).astype(BF16)
    sorted_fresh = dot(order, fin[...].reshape(fr, fw)).astype(BF16)
    new = rows * steps
    fn = jnp.concatenate(
        [sorted_fresh[c * new : (c + 1) * new, :] for c in range(8)], axis=1
    )
    f_step = iota((new, 1), 0) // rows
    f_cos = jnp.zeros((new, HD), F32)
    f_sin = jnp.zeros((new, HD), F32)
    bc = CTX // SPAN
    for t in range(steps):
        c0, s0 = tab_v[bc : bc + 1, :], tab_v[nb + bc : nb + bc + 1, :]
        c1, s1 = tok_cos[t : t + 1, :], tok_sin[t : t + 1, :]
        f_cos = jnp.where(f_step == t, c0 * c1 - s0 * s1, f_cos)
        f_sin = jnp.where(f_step == t, s0 * c1 + c0 * s1, f_sin)
    raw = dot(fn, wk[...])
    fk = jnp.concatenate([turn(b, f_cos, f_sin) for b in per_head(raw, heads)], axis=1).astype(BF16)
    fv = dot(fn, wv[...]).astype(BF16)

    near = rk.shape[0]
    resident = near // rows
    rk_copy.wait()
    rv_copy.wait()
    in_row = iota((inner, 1), 0)
    in_head = in_row // rows % heads
    q_near = spread_heads(q64, heads, in_head).astype(BF16)
    lane_near = iota((1, near), 1)
    col_row = jnp.full((1, near), -1, jnp.int32)
    for r in range(rows):
        ok = (lane_near >= r * resident) & (lane_near < r * resident + len_s[r])
        col_row = jnp.where(ok, r, col_row)
    live_near = col_row == in_row % rows
    lane_new = iota((1, new), 1)
    live_new = (lane_new % rows == in_row % rows) & (lane_new // rows <= in_row // (rows * heads))
    s_near = jnp.where(live_near, dot_nt(q_near, rk[...]) * scale, NEG)
    s_new = jnp.where(live_new, dot_nt(q_near, fk) * scale, NEG)
    peak_n = jnp.maximum(
        jnp.max(s_near, axis=1, keepdims=True), jnp.max(s_new, axis=1, keepdims=True)
    )
    p_near = jnp.where(live_near, jnp.exp(s_near - peak_n), 0.0)
    p_new = jnp.where(live_new, jnp.exp(s_new - peak_n), 0.0)
    total_n = jnp.sum(p_near, axis=1, keepdims=True) + jnp.sum(p_new, axis=1, keepdims=True)
    o_near = own_head(
        dot(p_near.astype(BF16), rv[...]) + dot(p_new.astype(BF16), fv), heads, in_head
    )

    from_all = pltpu.make_async_remote_copy(
        src_ref=pob.at[pl.ds(0, engines - 1)],
        dst_ref=pib.at[pl.ds(0, engines - 1)],
        send_sem=sem_p.at[0],
        recv_sem=sem_p.at[1],
        device_id=(me, z),
        device_id_type=MESH,
    )
    from_all.wait_recv()
    pin = pib[...].astype(F32)
    o_in = pin[:, :sh, :].reshape(pairs, HD)
    parts = pin[:, sh:, :].reshape(pairs, HD)
    lse_in = parts[:, 0:1] + parts[:, 32:33] + parts[:, 64:65]
    eye = iota((inner, inner), 0) == iota((inner, inner), 1)
    peak_lane = jnp.sum(jnp.where(eye, peak_n, 0.0), axis=0, keepdims=True)
    top = jnp.maximum(
        jnp.max(jnp.where(pick, lse_in, NEG), axis=0, keepdims=True), peak_lane
    )
    top_pair = jnp.sum(jnp.where(pick, top, 0.0), axis=1, keepdims=True)
    top_in = jnp.sum(jnp.where(eye, top, 0.0), axis=1, keepdims=True)
    valid = row_col > 0.0
    w_in = jnp.where(valid, jnp.exp(jnp.where(valid, lse_in - top_pair, 0.0)), 0.0)
    weighted = jnp.concatenate(
        [jnp.where(valid, w_in * o_in, 0.0), jnp.broadcast_to(w_in, (pairs, HD))], axis=1
    )
    first = weighted.astype(BF16)
    second = (weighted - first.astype(F32)).astype(BF16)
    collect = jnp.where(pick_t, 1.0, 0.0).astype(BF16)
    gathered = dot(collect, first) + dot(collect, second)
    w_near = jnp.exp(peak_n - top_in)
    result = (w_near * o_near + gathered[:, :HD]) / (w_near * total_n + gathered[:, HD:])
    for t in range(steps):
        for h in range(heads):
            j = t * heads + h
            out_v[t, :, h * HD : (h + 1) * HD] = result[j * rows : (j + 1) * rows, :].astype(BF16)

    everyone.wait_send()
    fresh_all.wait_send()
    from_all.wait_send()


def per_device(
    engines,
    tps,
    outgoing,
    span_target,
    span_row,
    span_block,
    span_tokens,
    norm_gain,
    key_weight,
    value_weight,
    fresh_states,
    queries,
    res_keys,
    res_values,
    res_len,
):
    sends, span, depth = outgoing.shape
    width = key_weight.shape[1]
    steps, rows, _ = queries.shape
    resident = res_keys.shape[1]
    heads = width // HD
    sh = steps * heads
    tokens = sends * span
    vmem = pl.BlockSpec(memory_space=pltpu.VMEM)
    hbm = pl.BlockSpec(memory_space=pltpu.HBM)
    chunks = 8
    table = jnp.asarray(rope_tables(steps))
    return pl.pallas_call(
        functools.partial(kernel, engines, tps, sends, rows, steps),
        out_shape=jax.ShapeDtypeStruct((steps, rows, width), BF16),
        in_specs=[hbm] * 14,
        out_specs=vmem,
        scratch_shapes=[
            pltpu.VMEM((tokens, depth), BF16),
            pltpu.VMEM((tokens, depth), BF16),
            pltpu.VMEM((depth, width), BF16),
            pltpu.VMEM((depth, width), BF16),
            pltpu.VMEM((rows * resident, width), BF16),
            pltpu.VMEM((rows * resident, width), BF16),
            pltpu.VMEM((tokens, width), F32),
            pltpu.VMEM((tokens, width), F32),
            pltpu.VMEM((tokens, width), BF16),
            pltpu.VMEM((tokens, width), BF16),
            pltpu.VMEM((tokens, HD), F32),
            pltpu.VMEM((tokens, HD), F32),
            pltpu.VMEM((tokens, HD), F32),
            pltpu.VMEM((steps * 8, depth // 8), F32),
            pltpu.VMEM((steps * 8, depth // 8), BF16),
            pltpu.VMEM((tps, steps * 8, depth // 8), BF16),
            pltpu.VMEM((engines, sh, HD), F32),
            pltpu.VMEM((engines, sh, HD), F32),
            pltpu.VMEM((engines, 2 * sh, HD), BF16),
            pltpu.VMEM((engines, 2 * sh, HD), BF16),
            pltpu.VMEM((engines * sh, sends * sh), BF16),
            pltpu.SMEM((sends, engines), jnp.int32),
            pltpu.SMEM((sends, engines), jnp.int32),
            pltpu.SMEM((sends, engines), jnp.int32),
            pltpu.SMEM((rows,), jnp.int32),
            pltpu.VMEM((sends, engines), jnp.int32),
            pltpu.VMEM((sends, engines), jnp.int32),
            pltpu.VMEM((1, depth), F32),
            pltpu.VMEM(table.shape, F32),
            pltpu.VMEM((steps, depth), BF16),
            pltpu.VMEM((steps, rows, width), BF16),
            pltpu.SemaphoreType.DMA((chunks,)),
            pltpu.SemaphoreType.DMA((2, chunks)),
            pltpu.SemaphoreType.DMA((2,)),
            pltpu.SemaphoreType.DMA((10,)),
            pltpu.SemaphoreType.DMA((2,)),
            pltpu.SemaphoreType.DMA((2,)),
            pltpu.SemaphoreType.DMA((2,)),
        ],
        compiler_params=pltpu.CompilerParams(
            collective_id=0, has_side_effects=True, vmem_limit_bytes=60 * 1024 * 1024
        ),
    )(
        outgoing.reshape(tokens, depth),
        span_target.T,
        span_row.T,
        span_block.T,
        span_tokens.T,
        res_len,
        norm_gain.reshape(1, depth),
        table,
        fresh_states.reshape(steps, depth),
        queries,
        key_weight,
        value_weight,
        res_keys.reshape(rows * resident, width),
        res_values.reshape(rows * resident, width),
    )


def solution(mesh):
    in_specs = (
        P("engine", None, None),
        P(),
        P(),
        P(),
        P(),
        P(),
        P(None, "tp"),
        P(None, "tp"),
        P(None, ("engine", "tp"), None),
        P(None, "engine", "tp"),
        P("engine", None, "tp"),
        P("engine", None, "tp"),
        P("engine"),
    )
    return jax.shard_map(
        functools.partial(per_device, mesh.shape["engine"], mesh.shape["tp"]),
        mesh=mesh,
        in_specs=in_specs,
        out_specs=P(None, "engine", "tp"),
        check_vma=False,
    )
```

```python
import functools
import math

import jax
import jax.numpy as jnp
import numpy as np
from jax import lax
from jax.experimental import pallas as pl
from jax.experimental.pallas import tpu as pltpu
from jax.sharding import PartitionSpec as P

MESH = pl.DeviceIdType.MESH
F32 = jnp.float32
BF16 = jnp.bfloat16
HD = 128
HALF = HD // 2
CTX = 2048
SPAN = 32
ROPE_BASE = 1000000.0
NORM_EPS = 1e-06
NEG = -1e30


def iota(shape, axis):
    return lax.broadcasted_iota(jnp.int32, shape, axis)


def rope_tables(steps):
    frequency = ROPE_BASE ** (-2.0 * np.arange(HALF) / HD)
    blocks = np.arange(CTX // SPAN + 8)[:, None] * SPAN * frequency[None, :]
    tokens = np.arange(SPAN)[:, None] * frequency[None, :]

    def wide(angles):
        cosine, sine = np.cos(angles), np.sin(angles)
        return np.concatenate([cosine, cosine], 1), np.concatenate([-sine, sine], 1)

    return np.concatenate([*wide(blocks), *wide(tokens)], 0).astype(np.float32)


def chunk_bounds(depth):
    edges = [depth * eighths // 8 for eighths in (0, 1, 3, 5, 7, 8)]
    return list(zip(edges[:-1], edges[1:], strict=True))


def far_first(engines):
    side = max(1, round(math.sqrt(engines // 2)))
    if side * side * 2 != engines:
        return [(0, 0, 0, i) for i in range(1, engines)]
    steps = [(x, y, c) for x in range(side) for y in range(side) for c in range(2)][1:]
    hops = lambda p: 2 * (min(p[0], side - p[0]) + min(p[1], side - p[1])) + p[2]
    return [(side, *p) for p in sorted(steps, key=hops, reverse=True)]


def dot(a, b):
    return jnp.dot(a, b, preferred_element_type=F32)


def dot_nt(a, b):
    return lax.dot_general(a, b, (((1,), (1,)), ((), ())), preferred_element_type=F32)


def per_head(x, count):
    return [x[:, h * HD : (h + 1) * HD] for h in range(count)]


def own_head(x, heads, head_of_row):
    blocks = per_head(x, heads)
    out = blocks[0]
    for h in range(1, heads):
        out = jnp.where(head_of_row == h, blocks[h], out)
    return out


def spread_heads(x, heads, head_of_row):
    return jnp.concatenate(
        [jnp.where(head_of_row == h, x, 0.0) for h in range(heads)], axis=1
    )


def kernel(
    engines,
    tps,
    sends,
    rows,
    steps,
    x_hbm,
    tgt_hbm,
    row_hbm,
    blk_hbm,
    tok_hbm,
    len_hbm,
    gain_hbm,
    tab_hbm,
    fresh_hbm,
    q_hbm,
    wk_hbm,
    wv_hbm,
    rk_hbm,
    rv_hbm,
    out_v,
    xv,
    nv,
    wk,
    wv,
    rk,
    rv,
    ak,
    av,
    kb,
    vb,
    squares,
    cosv,
    sinv,
    fst32,
    fst,
    fin,
    qob,
    qib,
    pob,
    pib,
    place,
    tgt_s,
    blk_s,
    tok_s,
    len_s,
    tgt_v,
    row_v,
    gain_v,
    tab_v,
    fresh_v,
    q_v,
    sem_x,
    sem_w,
    sem_r,
    sem_s,
    here,
    sem_f,
    sem_q,
    sem_p,
):
    me = lax.axis_index("engine")
    z = lax.axis_index("tp")
    order = far_first(engines)

    def partner(step):
        side, dx, dy, dc = step
        if side == 0:
            return lax.rem(me + dc, engines)
        x, y, core = me // (2 * side), me // 2 % side, me % 2
        return (lax.rem(x + dx, side) * side + lax.rem(y + dy, side)) * 2 + lax.rem(core + dc, 2)

    width = wk.shape[1]
    depth = wk.shape[0]
    heads = width // HD
    sh = steps * heads
    pairs = engines * sh
    inner = sh * rows
    tokens = sends * SPAN
    bounds = chunk_bounds(depth)
    chunks = len(bounds)

    def x_copy(c):
        part = pl.ds(bounds[c][0], bounds[c][1] - bounds[c][0])
        return pltpu.make_async_copy(x_hbm.at[:, part], xv.at[:, part], sem_x.at[c])

    def w_copy(m, c):
        part = pl.ds(bounds[c][0], bounds[c][1] - bounds[c][0])
        source, target = ((wk_hbm, wk), (wv_hbm, wv))[m]
        return pltpu.make_async_copy(source.at[part], target.at[part], sem_w.at[m, c])

    small = [
        pltpu.make_async_copy(source, target, sem_s.at[i])
        for i, (source, target) in enumerate(
            (
                (gain_hbm, gain_v),
                (fresh_hbm, fresh_v),
                (q_hbm, q_v),
                (tgt_hbm, tgt_v),
                (row_hbm, row_v),
                (tgt_hbm, tgt_s),
                (blk_hbm, blk_s),
                (tok_hbm, tok_s),
                (tab_hbm, tab_v),
                (len_hbm, len_s),
            )
        )
    ]
    for copy in small:
        copy.start()

    def start_chunk(c):
        x_copy(c).start()
        w_copy(0, c).start()
        w_copy(1, c).start()

    start_chunk(0)

    barrier = pltpu.get_barrier_semaphore()

    for step in order:
        pl.semaphore_signal(
            barrier, inc=1, device_id=(partner(step), z), device_id_type=MESH
        )

    def greet_higher(other, carry):
        pl.semaphore_signal(barrier, inc=1, device_id=(me, other), device_id_type=MESH)
        return carry

    lax.fori_loop(z + 1, tps, greet_higher, 0)

    for c in range(1, chunks):
        start_chunk(c)
    rk_copy = pltpu.make_async_copy(rk_hbm, rk, sem_r.at[0])
    rv_copy = pltpu.make_async_copy(rv_hbm, rv, sem_r.at[1])
    rk_copy.start()
    rv_copy.start()

    def turn(raw, cosine, sine):
        return raw * cosine + pltpu.roll(raw, HALF, 1) * sine

    def prepare(c):
        for j in range(bounds[c][0] // HD, bounds[c][1] // HD):
            lanes = slice(j * HD, (j + 1) * HD)
            block = xv[:, lanes].astype(F32)
            nv[:, lanes] = (block * gain_v[j : j + 1, :]).astype(BF16)
            square = block * block
            folded = square if j == bounds[c][0] // HD else folded + square
        squares[...] = folded if c == 0 else squares[...] + folded

    def multiply(c):
        part = slice(*bounds[c])
        for weight, total in ((wk, ak), (wv, av)):
            raw = dot(nv[:, part], weight[part, :])
            total[...] = raw if c == 0 else total[...] + raw

    def wait_chunk(c):
        x_copy(c).wait()
        w_copy(0, c).wait()
        w_copy(1, c).wait()

    for copy in small:
        copy.wait()

    q = q_v[...].astype(F32)
    q64 = jnp.concatenate(
        [q[s][:, h * HD : (h + 1) * HD] for s in range(steps) for h in range(heads)], axis=0
    )
    hit = tgt_v[...] == me
    arrives = jnp.sum(jnp.where(hit, (row_v[...] + 1).astype(F32), 0.0), axis=0, keepdims=True)
    pe = iota((pairs, engines), 0) // sh
    row_col = jnp.sum(
        jnp.where(pe == iota((pairs, engines), 1), arrives, 0.0), axis=1, keepdims=True
    )
    arr_col = jnp.sum(
        jnp.where(
            iota((engines, engines), 0) == iota((engines, engines), 1), arrives, 0.0
        ),
        axis=1,
        keepdims=True,
    )
    row_lane = jnp.sum(
        jnp.where(
            iota((engines, pairs), 0) == iota((engines, pairs), 1) // sh, arr_col, 0.0
        ),
        axis=0,
        keepdims=True,
    )
    gi, gl = iota((pairs, inner), 0), iota((pairs, inner), 1)
    pick = (row_col == (gl % rows + 1).astype(F32)) & (gi % sh == gl // rows)
    ti, tl = iota((inner, pairs), 0), iota((inner, pairs), 1)
    pick_t = (row_lane == (ti % rows + 1).astype(F32)) & (tl % sh == ti // rows)
    qout = dot(jnp.where(pick, 1.0, 0.0).astype(BF16), q64.astype(BF16))
    qob[...] = qout.reshape(engines, sh, HD)
    qib[me] = jnp.zeros((sh, HD), F32)


    def q_copy(step):
        other = partner(step)
        return pltpu.make_async_remote_copy(
            src_ref=qob.at[other],
            dst_ref=qib.at[me],
            send_sem=sem_q.at[0],
            recv_sem=sem_q.at[1],
            device_id=(other, z),
            device_id_type=MESH,
        )

    pl.semaphore_wait(barrier, engines - 1 + z)
    for step in order:
        q_copy(step).start()

    fw = depth // 8
    fresh = fresh_v[...].astype(F32)
    fresh = fresh * lax.rsqrt(jnp.mean(fresh * fresh, axis=1, keepdims=True) + NORM_EPS)
    for s in range(steps):
        for j in range(depth // HD):
            row, at = s * 8 + j * HD // fw, j * HD % fw
            fst32[row : row + 1, at : at + HD] = (
                fresh[s : s + 1, j * HD : (j + 1) * HD] * gain_v[j : j + 1, :]
            )
    fst[...] = fst32[...].astype(BF16)
    fin[z] = fst[...]


    def f_copy(other):
        return pltpu.make_async_remote_copy(
            src_ref=fst,
            dst_ref=fin.at[z],
            send_sem=sem_f.at[0],
            recv_sem=sem_f.at[1],
            device_id=(me, other),
            device_id_type=MESH,
        )

    def answer_lower(other, carry):
        pl.semaphore_signal(here, inc=1, device_id=(me, other), device_id_type=MESH)
        f_copy(other).start()
        return carry

    def send_higher(other, carry):
        f_copy(other).start()
        return carry

    lax.fori_loop(0, z, answer_lower, 0)

    wait_chunk(0)
    prepare(0)
    multiply(0)

    wait_chunk(1)
    prepare(1)
    multiply(1)

    nb = CTX // SPAN + 8
    tok_cos = tab_v[2 * nb : 2 * nb + SPAN, :]
    tok_sin = tab_v[2 * nb + SPAN : 2 * nb + 2 * SPAN, :]
    span_lane = iota((1, sends * sh), 1)
    lane_target = jnp.full((1, sends * sh), -1, jnp.int32)
    for k in range(sends):
        b = blk_s[k, me]
        block_cos = tab_v[pl.ds(b, 1), :]
        block_sin = tab_v[pl.ds(b + nb, 1), :]
        cosv[k * SPAN : (k + 1) * SPAN, :] = block_cos * tok_cos - block_sin * tok_sin
        sinv[k * SPAN : (k + 1) * SPAN, :] = block_sin * tok_cos + block_cos * tok_sin
        lane_target = jnp.where(span_lane // sh == k, tgt_s[k, me], lane_target)
    oi, ol = iota((pairs, sends * sh), 0), iota((pairs, sends * sh), 1)
    place[...] = jnp.where((lane_target == oi // sh) & (oi % sh == ol % sh), 1.0, 0.0).astype(BF16)

    for c in range(2, chunks):
        wait_chunk(c)
        prepare(c)
        multiply(c)
    mean = jnp.sum(squares[...], axis=1, keepdims=True) * (1.0 / depth)
    factor = lax.rsqrt(mean + NORM_EPS)
    cosine = cosv[...] * factor
    sine = sinv[...] * factor
    for h in range(heads):
        head = slice(h * HD, (h + 1) * HD)
        kb[:, head] = turn(ak[:, head], cosine, sine).astype(BF16)
    vb[...] = (av[...] * factor).astype(BF16)

    scale = 1.0 / math.sqrt(HD)
    everyone = pltpu.make_async_remote_copy(
        src_ref=qob.at[pl.ds(0, engines - 1)],
        dst_ref=qib.at[pl.ds(0, engines - 1)],
        send_sem=sem_q.at[0],
        recv_sem=sem_q.at[1],
        device_id=(me, z),
        device_id_type=MESH,
    )
    everyone.wait_recv()
    made = []
    for g in range(0, sends, HD // SPAN):
        spans = range(g, min(g + HD // SPAN, sends))
        count = len(spans)
        group = slice(g * SPAN, (g + count) * SPAN)
        q_g = jnp.concatenate([qib[tgt_s[k, me]] for k in spans], axis=0)
        g_row = iota((count * sh, 1), 0)
        g_lane = iota((1, count * SPAN), 1)
        edge = jnp.zeros((count * sh, 1), jnp.int32)
        for j, k in enumerate(spans):
            edge = jnp.where(g_row // sh == j, j * SPAN + tok_s[k, me], edge)
        live = (g_lane >= g_row // sh * SPAN) & (g_lane < edge)
        s = dot_nt(spread_heads(q_g, heads, g_row % heads).astype(BF16), kb[group, :]) * scale
        s = jnp.where(live, s, NEG)
        peak = jnp.max(s, axis=1, keepdims=True)
        p = jnp.where(live, jnp.exp(s - peak), 0.0)
        total = jnp.sum(p, axis=1, keepdims=True)
        o = own_head(dot(p.astype(BF16), vb[group, :]), heads, g_row % heads) / total
        lse = peak + jnp.log(total)
        hi = lse.astype(BF16).astype(F32)
        mid = (lse - hi).astype(BF16).astype(F32)
        low = lse - hi - mid
        lane = iota((count * sh, HD), 1)
        coded = jnp.where(lane < 32, hi, jnp.where(lane < 64, mid, low))
        made.append(jnp.concatenate([o, coded], axis=1).astype(BF16))
    placed = dot(place[...], jnp.concatenate(made, axis=0))
    pob[...] = jnp.concatenate(
        [placed[:, :HD].reshape(engines, sh, HD), placed[:, HD:].reshape(engines, sh, HD)], axis=1
    ).astype(BF16)

    def p_copy(step):
        other = partner(step)
        return pltpu.make_async_remote_copy(
            src_ref=pob.at[other],
            dst_ref=pib.at[me],
            send_sem=sem_p.at[0],
            recv_sem=sem_p.at[1],
            device_id=(other, z),
            device_id_type=MESH,
        )

    for step in order:
        p_copy(step).start()
    pib[me] = jnp.zeros((2 * sh, HD), BF16)

    @pl.when(z < tps - 1)
    def _():
        pl.semaphore_wait(here, tps - 1 - z)

    lax.fori_loop(z + 1, tps, send_higher, 0)

    fresh_all = pltpu.make_async_remote_copy(
        src_ref=fin.at[pl.ds(0, tps - 1)],
        dst_ref=fin.at[pl.ds(0, tps - 1)],
        send_sem=sem_f.at[0],
        recv_sem=sem_f.at[1],
        device_id=(me, z),
        device_id_type=MESH,
    )
    fresh_all.wait_recv()
    fr = rows * steps * 8
    ri, rl = iota((fr, fr), 0), iota((fr, fr), 1)
    want = (ri % rows) * (steps * 8) + (ri // rows % steps) * 8 + ri // (rows * steps)
    order = jnp.where(rl == want, 1.0, 0.0).astype(BF16)
    sorted_fresh = dot(order, fin[...].reshape(fr, fw)).astype(BF16)
    new = rows * steps
    fn = jnp.concatenate(
        [sorted_fresh[c * new : (c + 1) * new, :] for c in range(8)], axis=1
    )
    f_step = iota((new, 1), 0) // rows
    f_cos = jnp.zeros((new, HD), F32)
    f_sin = jnp.zeros((new, HD), F32)
    bc = CTX // SPAN
    for t in range(steps):
        c0, s0 = tab_v[bc : bc + 1, :], tab_v[nb + bc : nb + bc + 1, :]
        c1, s1 = tok_cos[t : t + 1, :], tok_sin[t : t + 1, :]
        f_cos = jnp.where(f_step == t, c0 * c1 - s0 * s1, f_cos)
        f_sin = jnp.where(f_step == t, s0 * c1 + c0 * s1, f_sin)
    raw = dot(fn, wk[...])
    fk = jnp.concatenate([turn(b, f_cos, f_sin) for b in per_head(raw, heads)], axis=1).astype(BF16)
    fv = dot(fn, wv[...]).astype(BF16)

    near = rk.shape[0]
    resident = near // rows
    rk_copy.wait()
    rv_copy.wait()
    in_row = iota((inner, 1), 0)
    in_head = in_row // rows % heads
    q_near = spread_heads(q64, heads, in_head).astype(BF16)
    lane_near = iota((1, near), 1)
    col_row = jnp.full((1, near), -1, jnp.int32)
    for r in range(rows):
        ok = (lane_near >= r * resident) & (lane_near < r * resident + len_s[r])
        col_row = jnp.where(ok, r, col_row)
    live_near = col_row == in_row % rows
    lane_new = iota((1, new), 1)
    live_new = (lane_new % rows == in_row % rows) & (lane_new // rows <= in_row // (rows * heads))
    s_near = jnp.where(live_near, dot_nt(q_near, rk[...]) * scale, NEG)
    s_new = jnp.where(live_new, dot_nt(q_near, fk) * scale, NEG)
    peak_n = jnp.maximum(
        jnp.max(s_near, axis=1, keepdims=True), jnp.max(s_new, axis=1, keepdims=True)
    )
    p_near = jnp.where(live_near, jnp.exp(s_near - peak_n), 0.0)
    p_new = jnp.where(live_new, jnp.exp(s_new - peak_n), 0.0)
    total_n = jnp.sum(p_near, axis=1, keepdims=True) + jnp.sum(p_new, axis=1, keepdims=True)
    o_near = own_head(
        dot(p_near.astype(BF16), rv[...]) + dot(p_new.astype(BF16), fv), heads, in_head
    )

    from_all = pltpu.make_async_remote_copy(
        src_ref=pob.at[pl.ds(0, engines - 1)],
        dst_ref=pib.at[pl.ds(0, engines - 1)],
        send_sem=sem_p.at[0],
        recv_sem=sem_p.at[1],
        device_id=(me, z),
        device_id_type=MESH,
    )
    from_all.wait_recv()
    pin = pib[...].astype(F32)
    o_in = pin[:, :sh, :].reshape(pairs, HD)
    parts = pin[:, sh:, :].reshape(pairs, HD)
    lse_in = parts[:, 0:1] + parts[:, 32:33] + parts[:, 64:65]
    eye = iota((inner, inner), 0) == iota((inner, inner), 1)
    peak_lane = jnp.sum(jnp.where(eye, peak_n, 0.0), axis=0, keepdims=True)
    top = jnp.maximum(
        jnp.max(jnp.where(pick, lse_in, NEG), axis=0, keepdims=True), peak_lane
    )
    top_pair = jnp.sum(jnp.where(pick, top, 0.0), axis=1, keepdims=True)
    top_in = jnp.sum(jnp.where(eye, top, 0.0), axis=1, keepdims=True)
    valid = row_col > 0.0
    w_in = jnp.where(valid, jnp.exp(jnp.where(valid, lse_in - top_pair, 0.0)), 0.0)
    weighted = jnp.concatenate(
        [jnp.where(valid, w_in * o_in, 0.0), jnp.broadcast_to(w_in, (pairs, HD))], axis=1
    )
    first = weighted.astype(BF16)
    second = (weighted - first.astype(F32)).astype(BF16)
    collect = jnp.where(pick_t, 1.0, 0.0).astype(BF16)
    gathered = dot(collect, first) + dot(collect, second)
    w_near = jnp.exp(peak_n - top_in)
    result = (w_near * o_near + gathered[:, :HD]) / (w_near * total_n + gathered[:, HD:])
    for t in range(steps):
        for h in range(heads):
            j = t * heads + h
            out_v[t, :, h * HD : (h + 1) * HD] = result[j * rows : (j + 1) * rows, :].astype(BF16)

    everyone.wait_send()
    fresh_all.wait_send()
    from_all.wait_send()


def per_device(
    engines,
    tps,
    outgoing,
    span_target,
    span_row,
    span_block,
    span_tokens,
    norm_gain,
    key_weight,
    value_weight,
    fresh_states,
    queries,
    res_keys,
    res_values,
    res_len,
):
    sends, span, depth = outgoing.shape
    width = key_weight.shape[1]
    steps, rows, _ = queries.shape
    resident = res_keys.shape[1]
    heads = width // HD
    sh = steps * heads
    tokens = sends * span
    vmem = pl.BlockSpec(memory_space=pltpu.VMEM)
    hbm = pl.BlockSpec(memory_space=pltpu.HBM)
    chunks = len(chunk_bounds(depth))
    table = jnp.asarray(rope_tables(steps))
    return pl.pallas_call(
        functools.partial(kernel, engines, tps, sends, rows, steps),
        out_shape=jax.ShapeDtypeStruct((steps, rows, width), BF16),
        in_specs=[hbm] * 14,
        out_specs=vmem,
        scratch_shapes=[
            pltpu.VMEM((tokens, depth), BF16),
            pltpu.VMEM((tokens, depth), BF16),
            pltpu.VMEM((depth, width), BF16),
            pltpu.VMEM((depth, width), BF16),
            pltpu.VMEM((rows * resident, width), BF16),
            pltpu.VMEM((rows * resident, width), BF16),
            pltpu.VMEM((tokens, width), F32),
            pltpu.VMEM((tokens, width), F32),
            pltpu.VMEM((tokens, width), BF16),
            pltpu.VMEM((tokens, width), BF16),
            pltpu.VMEM((tokens, HD), F32),
            pltpu.VMEM((tokens, HD), F32),
            pltpu.VMEM((tokens, HD), F32),
            pltpu.VMEM((steps * 8, depth // 8), F32),
            pltpu.VMEM((steps * 8, depth // 8), BF16),
            pltpu.VMEM((tps, steps * 8, depth // 8), BF16),
            pltpu.VMEM((engines, sh, HD), F32),
            pltpu.VMEM((engines, sh, HD), F32),
            pltpu.VMEM((engines, 2 * sh, HD), BF16),
            pltpu.VMEM((engines, 2 * sh, HD), BF16),
            pltpu.VMEM((engines * sh, sends * sh), BF16),
            pltpu.SMEM((sends, engines), jnp.int32),
            pltpu.SMEM((sends, engines), jnp.int32),
            pltpu.SMEM((sends, engines), jnp.int32),
            pltpu.SMEM((rows,), jnp.int32),
            pltpu.VMEM((sends, engines), jnp.int32),
            pltpu.VMEM((sends, engines), jnp.int32),
            pltpu.VMEM((depth // HD, HD), F32),
            pltpu.VMEM(table.shape, F32),
            pltpu.VMEM((steps, depth), BF16),
            pltpu.VMEM((steps, rows, width), BF16),
            pltpu.SemaphoreType.DMA((chunks,)),
            pltpu.SemaphoreType.DMA((2, chunks)),
            pltpu.SemaphoreType.DMA((2,)),
            pltpu.SemaphoreType.DMA((10,)),
            pltpu.SemaphoreType.REGULAR,
            pltpu.SemaphoreType.DMA((2,)),
            pltpu.SemaphoreType.DMA((2,)),
            pltpu.SemaphoreType.DMA((2,)),
        ],
        compiler_params=pltpu.CompilerParams(
            collective_id=0, has_side_effects=True, vmem_limit_bytes=60 * 1024 * 1024
        ),
    )(
        outgoing.reshape(tokens, depth),
        span_target.T,
        span_row.T,
        span_block.T,
        span_tokens.T,
        res_len,
        norm_gain.reshape(depth // HD, HD),
        table,
        fresh_states.reshape(steps, depth),
        queries,
        key_weight,
        value_weight,
        res_keys.reshape(rows * resident, width),
        res_values.reshape(rows * resident, width),
    )


def solution(mesh):
    in_specs = (
        P("engine", None, None),
        P(),
        P(),
        P(),
        P(),
        P(),
        P(None, "tp"),
        P(None, "tp"),
        P(None, ("engine", "tp"), None),
        P(None, "engine", "tp"),
        P("engine", None, "tp"),
        P("engine", None, "tp"),
        P("engine"),
    )
    return jax.shard_map(
        functools.partial(per_device, mesh.shape["engine"], mesh.shape["tp"]),
        mesh=mesh,
        in_specs=in_specs,
        out_specs=P(None, "engine", "tp"),
        check_vma=False,
    )
```

```python
import functools
import math

import jax
import jax.numpy as jnp
import numpy as np
from jax import lax
from jax.experimental import pallas as pl
from jax.experimental.pallas import tpu as pltpu
from jax.sharding import PartitionSpec as P

MESH = pl.DeviceIdType.MESH
F32 = jnp.float32
BF16 = jnp.bfloat16
HD = 128
HALF = HD // 2
CTX = 2048
SPAN = 32
ROPE_BASE = 1000000.0
NORM_EPS = 1e-06
NEG = -1e30


def iota(shape, axis):
    return lax.broadcasted_iota(jnp.int32, shape, axis)


def rope_tables(steps):
    frequency = ROPE_BASE ** (-2.0 * np.arange(HALF) / HD)
    blocks = np.arange(CTX // SPAN + 8)[:, None] * SPAN * frequency[None, :]
    tokens = np.arange(SPAN)[:, None] * frequency[None, :]

    def wide(angles):
        cosine, sine = np.cos(angles), np.sin(angles)
        return np.concatenate([cosine, cosine], 1), np.concatenate([-sine, sine], 1)

    return np.concatenate([*wide(blocks), *wide(tokens)], 0).astype(np.float32)


def chunk_bounds(depth):
    edges = [depth * eighths // 8 for eighths in (0, 1, 3, 5, 7, 8)]
    return list(zip(edges[:-1], edges[1:], strict=True))


def far_first(engines):
    side = max(1, round(math.sqrt(engines // 2)))
    if side * side * 2 != engines:
        return [(0, 0, 0, i) for i in range(1, engines)]
    steps = [(x, y, c) for x in range(side) for y in range(side) for c in range(2)][1:]
    hops = lambda p: 2 * (min(p[0], side - p[0]) + min(p[1], side - p[1])) + p[2]
    return [(side, *p) for p in sorted(steps, key=hops, reverse=True)]


def dot(a, b):
    return jnp.dot(a, b, preferred_element_type=F32)


def dot_nt(a, b):
    return lax.dot_general(a, b, (((1,), (1,)), ((), ())), preferred_element_type=F32)


def per_head(x, count):
    return [x[:, h * HD : (h + 1) * HD] for h in range(count)]


def own_head(x, heads, head_of_row):
    blocks = per_head(x, heads)
    out = blocks[0]
    for h in range(1, heads):
        out = jnp.where(head_of_row == h, blocks[h], out)
    return out


def spread_heads(x, heads, head_of_row):
    return jnp.concatenate(
        [jnp.where(head_of_row == h, x, 0.0) for h in range(heads)], axis=1
    )


def kernel(
    engines,
    tps,
    sends,
    rows,
    steps,
    x_hbm,
    tgt_hbm,
    row_hbm,
    blk_hbm,
    tok_hbm,
    len_hbm,
    gain_hbm,
    tab_hbm,
    fresh_hbm,
    q_hbm,
    wk_hbm,
    wv_hbm,
    rk_hbm,
    rv_hbm,
    out_v,
    xv,
    nv,
    wk,
    wv,
    rk,
    rv,
    ak,
    av,
    kb,
    vb,
    squares,
    cosv,
    sinv,
    fst32,
    fst,
    fin,
    qob,
    qib,
    pob,
    pib,
    place,
    tgt_s,
    blk_s,
    tok_s,
    len_s,
    tgt_v,
    row_v,
    gain_v,
    tab_v,
    fresh_v,
    q_v,
    sem_x,
    sem_w,
    sem_r,
    sem_s,
    here,
    sem_f,
    sem_q,
    sem_p,
):
    me = lax.axis_index("engine")
    z = lax.axis_index("tp")
    order = far_first(engines)

    def partner(step):
        side, dx, dy, dc = step
        if side == 0:
            return lax.rem(me + dc, engines)
        x, y, core = me // (2 * side), me // 2 % side, me % 2
        return (lax.rem(x + dx, side) * side + lax.rem(y + dy, side)) * 2 + lax.rem(core + dc, 2)

    width = wk.shape[1]
    depth = wk.shape[0]
    heads = width // HD
    sh = steps * heads
    pairs = engines * sh
    inner = sh * rows
    tokens = sends * SPAN
    bounds = chunk_bounds(depth)
    chunks = len(bounds)

    def x_copy(c):
        part = pl.ds(bounds[c][0], bounds[c][1] - bounds[c][0])
        return pltpu.make_async_copy(x_hbm.at[:, part], xv.at[:, part], sem_x.at[c])

    def w_copy(m, c):
        part = pl.ds(bounds[c][0], bounds[c][1] - bounds[c][0])
        source, target = ((wk_hbm, wk), (wv_hbm, wv))[m]
        return pltpu.make_async_copy(source.at[part], target.at[part], sem_w.at[m, c])

    barrier = pltpu.get_barrier_semaphore()
    for step in order:
        pl.semaphore_signal(
            barrier, inc=1, device_id=(partner(step), z), device_id_type=MESH
        )

    def greet_higher(other, carry):
        pl.semaphore_signal(barrier, inc=1, device_id=(me, other), device_id_type=MESH)
        return carry

    lax.fori_loop(z + 1, tps, greet_higher, 0)

    small = [
        pltpu.make_async_copy(source, target, sem_s.at[i])
        for i, (source, target) in enumerate(
            (
                (q_hbm, q_v),
                (tgt_hbm, tgt_v),
                (row_hbm, row_v),
                (gain_hbm, gain_v),
                (fresh_hbm, fresh_v),
                (tgt_hbm, tgt_s),
                (blk_hbm, blk_s),
                (tok_hbm, tok_s),
                (tab_hbm, tab_v),
                (len_hbm, len_s),
            )
        )
    ]
    for copy in small:
        copy.start()

    def start_chunk(c):
        x_copy(c).start()
        w_copy(0, c).start()
        w_copy(1, c).start()

    start_chunk(0)

    def turn(raw, cosine, sine):
        return raw * cosine + pltpu.roll(raw, HALF, 1) * sine

    def prepare(c):
        for j in range(bounds[c][0] // HD, bounds[c][1] // HD):
            lanes = slice(j * HD, (j + 1) * HD)
            block = xv[:, lanes].astype(F32)
            nv[:, lanes] = (block * gain_v[j : j + 1, :]).astype(BF16)
            square = block * block
            folded = square if j == bounds[c][0] // HD else folded + square
        squares[...] = folded if c == 0 else squares[...] + folded

    def multiply(c):
        part = slice(*bounds[c])
        for weight, total in ((wk, ak), (wv, av)):
            raw = dot(nv[:, part], weight[part, :])
            total[...] = raw if c == 0 else total[...] + raw

    def wait_chunk(c):
        x_copy(c).wait()
        w_copy(0, c).wait()
        w_copy(1, c).wait()

    for copy in small[:3]:
        copy.wait()
    q = q_v[...].astype(F32)
    q64 = jnp.concatenate(
        [q[s][:, h * HD : (h + 1) * HD] for s in range(steps) for h in range(heads)], axis=0
    )
    hit = tgt_v[...] == me
    arrives = jnp.sum(jnp.where(hit, (row_v[...] + 1).astype(F32), 0.0), axis=0, keepdims=True)
    pe = iota((pairs, engines), 0) // sh
    row_col = jnp.sum(
        jnp.where(pe == iota((pairs, engines), 1), arrives, 0.0), axis=1, keepdims=True
    )
    arr_col = jnp.sum(
        jnp.where(
            iota((engines, engines), 0) == iota((engines, engines), 1), arrives, 0.0
        ),
        axis=1,
        keepdims=True,
    )
    row_lane = jnp.sum(
        jnp.where(
            iota((engines, pairs), 0) == iota((engines, pairs), 1) // sh, arr_col, 0.0
        ),
        axis=0,
        keepdims=True,
    )
    gi, gl = iota((pairs, inner), 0), iota((pairs, inner), 1)
    pick = (row_col == (gl % rows + 1).astype(F32)) & (gi % sh == gl // rows)
    ti, tl = iota((inner, pairs), 0), iota((inner, pairs), 1)
    pick_t = (row_lane == (ti % rows + 1).astype(F32)) & (tl % sh == ti // rows)
    qout = dot(jnp.where(pick, 1.0, 0.0).astype(BF16), q64.astype(BF16))
    qob[...] = qout.reshape(engines, sh, HD)
    qib[me] = jnp.zeros((sh, HD), F32)


    def q_copy(step):
        other = partner(step)
        return pltpu.make_async_remote_copy(
            src_ref=qob.at[other],
            dst_ref=qib.at[me],
            send_sem=sem_q.at[0],
            recv_sem=sem_q.at[1],
            device_id=(other, z),
            device_id_type=MESH,
        )

    for c in range(1, chunks):
        start_chunk(c)
    rk_copy = pltpu.make_async_copy(rk_hbm, rk, sem_r.at[0])
    rv_copy = pltpu.make_async_copy(rv_hbm, rv, sem_r.at[1])
    rk_copy.start()
    rv_copy.start()


    small[3].wait()
    wait_chunk(0)
    prepare(0)
    multiply(0)

    for copy in small[4:]:
        copy.wait()

    fw = depth // 8
    fresh = fresh_v[...].astype(F32)
    fresh = fresh * lax.rsqrt(jnp.mean(fresh * fresh, axis=1, keepdims=True) + NORM_EPS)
    for s in range(steps):
        for j in range(depth // HD):
            row, at = s * 8 + j * HD // fw, j * HD % fw
            fst32[row : row + 1, at : at + HD] = (
                fresh[s : s + 1, j * HD : (j + 1) * HD] * gain_v[j : j + 1, :]
            )
    fst[...] = fst32[...].astype(BF16)
    fin[z] = fst[...]


    def f_copy(other):
        return pltpu.make_async_remote_copy(
            src_ref=fst,
            dst_ref=fin.at[z],
            send_sem=sem_f.at[0],
            recv_sem=sem_f.at[1],
            device_id=(me, other),
            device_id_type=MESH,
        )

    def answer_lower(other, carry):
        pl.semaphore_signal(here, inc=1, device_id=(me, other), device_id_type=MESH)
        f_copy(other).start()
        return carry

    def send_higher(other, carry):
        f_copy(other).start()
        return carry

    pl.semaphore_wait(barrier, engines - 1 + z)
    lax.fori_loop(0, z, answer_lower, 0)
    for step in order:
        q_copy(step).start()

    wait_chunk(1)
    prepare(1)
    multiply(1)

    nb = CTX // SPAN + 8
    tok_cos = tab_v[2 * nb : 2 * nb + SPAN, :]
    tok_sin = tab_v[2 * nb + SPAN : 2 * nb + 2 * SPAN, :]
    span_lane = iota((1, sends * sh), 1)
    lane_target = jnp.full((1, sends * sh), -1, jnp.int32)
    for k in range(sends):
        b = blk_s[k, me]
        block_cos = tab_v[pl.ds(b, 1), :]
        block_sin = tab_v[pl.ds(b + nb, 1), :]
        cosv[k * SPAN : (k + 1) * SPAN, :] = block_cos * tok_cos - block_sin * tok_sin
        sinv[k * SPAN : (k + 1) * SPAN, :] = block_sin * tok_cos + block_cos * tok_sin
        lane_target = jnp.where(span_lane // sh == k, tgt_s[k, me], lane_target)
    oi, ol = iota((pairs, sends * sh), 0), iota((pairs, sends * sh), 1)
    place[...] = jnp.where((lane_target == oi // sh) & (oi % sh == ol % sh), 1.0, 0.0).astype(BF16)

    for c in range(2, chunks):
        wait_chunk(c)
        prepare(c)
        multiply(c)
    mean = jnp.sum(squares[...], axis=1, keepdims=True) * (1.0 / depth)
    factor = lax.rsqrt(mean + NORM_EPS)
    cosine = cosv[...] * factor
    sine = sinv[...] * factor
    for h in range(heads):
        head = slice(h * HD, (h + 1) * HD)
        kb[:, head] = turn(ak[:, head], cosine, sine).astype(BF16)
    vb[...] = (av[...] * factor).astype(BF16)

    scale = 1.0 / math.sqrt(HD)
    everyone = pltpu.make_async_remote_copy(
        src_ref=qob.at[pl.ds(0, engines - 1)],
        dst_ref=qib.at[pl.ds(0, engines - 1)],
        send_sem=sem_q.at[0],
        recv_sem=sem_q.at[1],
        device_id=(me, z),
        device_id_type=MESH,
    )

    def reach_higher():
        @pl.when(z < tps - 1)
        def _():
            pl.semaphore_wait(here, tps - 1 - z)

        lax.fori_loop(z + 1, tps, send_higher, 0)

    @pl.when(z >= tps // 2)
    def _():
        reach_higher()

    everyone.wait_recv()
    made = []
    for g in range(0, sends, HD // SPAN):
        spans = range(g, min(g + HD // SPAN, sends))
        count = len(spans)
        group = slice(g * SPAN, (g + count) * SPAN)
        q_g = jnp.concatenate([qib[tgt_s[k, me]] for k in spans], axis=0)
        g_row = iota((count * sh, 1), 0)
        g_lane = iota((1, count * SPAN), 1)
        edge = jnp.zeros((count * sh, 1), jnp.int32)
        for j, k in enumerate(spans):
            edge = jnp.where(g_row // sh == j, j * SPAN + tok_s[k, me], edge)
        live = (g_lane >= g_row // sh * SPAN) & (g_lane < edge)
        s = dot_nt(spread_heads(q_g, heads, g_row % heads).astype(BF16), kb[group, :]) * scale
        s = jnp.where(live, s, NEG)
        peak = jnp.max(s, axis=1, keepdims=True)
        p = jnp.where(live, jnp.exp(s - peak), 0.0)
        total = jnp.sum(p, axis=1, keepdims=True)
        o = own_head(dot(p.astype(BF16), vb[group, :]), heads, g_row % heads) / total
        lse = peak + jnp.log(total)
        hi = lse.astype(BF16).astype(F32)
        mid = (lse - hi).astype(BF16).astype(F32)
        low = lse - hi - mid
        lane = iota((count * sh, HD), 1)
        coded = jnp.where(lane < 32, hi, jnp.where(lane < 64, mid, low))
        made.append(jnp.concatenate([o, coded], axis=1).astype(BF16))
    placed = dot(place[...], jnp.concatenate(made, axis=0))
    pob[...] = jnp.concatenate(
        [placed[:, :HD].reshape(engines, sh, HD), placed[:, HD:].reshape(engines, sh, HD)], axis=1
    ).astype(BF16)

    def p_copy(step):
        other = partner(step)
        return pltpu.make_async_remote_copy(
            src_ref=pob.at[other],
            dst_ref=pib.at[me],
            send_sem=sem_p.at[0],
            recv_sem=sem_p.at[1],
            device_id=(other, z),
            device_id_type=MESH,
        )

    for step in order:
        p_copy(step).start()
    pib[me] = jnp.zeros((2 * sh, HD), BF16)

    @pl.when(z < tps // 2)
    def _():
        reach_higher()

    near = rk.shape[0]
    resident = near // rows
    rk_copy.wait()
    rv_copy.wait()
    in_row = iota((inner, 1), 0)
    in_head = in_row // rows % heads
    q_near = spread_heads(q64, heads, in_head).astype(BF16)
    lane_near = iota((1, near), 1)
    col_row = jnp.full((1, near), -1, jnp.int32)
    for r in range(rows):
        ok = (lane_near >= r * resident) & (lane_near < r * resident + len_s[r])
        col_row = jnp.where(ok, r, col_row)
    live_near = col_row == in_row % rows
    s_near = jnp.where(live_near, dot_nt(q_near, rk[...]) * scale, NEG)
    peak_near = jnp.max(s_near, axis=1, keepdims=True)
    p_near = jnp.where(live_near, jnp.exp(s_near - peak_near), 0.0)
    total_near = jnp.sum(p_near, axis=1, keepdims=True)
    sum_near = own_head(dot(p_near.astype(BF16), rv[...]), heads, in_head)

    fresh_all = pltpu.make_async_remote_copy(
        src_ref=fin.at[pl.ds(0, tps - 1)],
        dst_ref=fin.at[pl.ds(0, tps - 1)],
        send_sem=sem_f.at[0],
        recv_sem=sem_f.at[1],
        device_id=(me, z),
        device_id_type=MESH,
    )
    fresh_all.wait_recv()
    fr = rows * steps * 8
    ri, rl = iota((fr, fr), 0), iota((fr, fr), 1)
    want = (ri % rows) * (steps * 8) + (ri // rows % steps) * 8 + ri // (rows * steps)
    order = jnp.where(rl == want, 1.0, 0.0).astype(BF16)
    sorted_fresh = dot(order, fin[...].reshape(fr, fw)).astype(BF16)
    new = rows * steps
    fn = jnp.concatenate(
        [sorted_fresh[c * new : (c + 1) * new, :] for c in range(8)], axis=1
    )
    f_step = iota((new, 1), 0) // rows
    f_cos = jnp.zeros((new, HD), F32)
    f_sin = jnp.zeros((new, HD), F32)
    bc = CTX // SPAN
    for t in range(steps):
        c0, s0 = tab_v[bc : bc + 1, :], tab_v[nb + bc : nb + bc + 1, :]
        c1, s1 = tok_cos[t : t + 1, :], tok_sin[t : t + 1, :]
        f_cos = jnp.where(f_step == t, c0 * c1 - s0 * s1, f_cos)
        f_sin = jnp.where(f_step == t, s0 * c1 + c0 * s1, f_sin)
    raw = dot(fn, wk[...])
    fk = jnp.concatenate([turn(b, f_cos, f_sin) for b in per_head(raw, heads)], axis=1).astype(BF16)
    fv = dot(fn, wv[...]).astype(BF16)

    lane_new = iota((1, new), 1)
    live_new = (lane_new % rows == in_row % rows) & (lane_new // rows <= in_row // (rows * heads))
    s_new = jnp.where(live_new, dot_nt(q_near, fk) * scale, NEG)
    peak_n = jnp.maximum(peak_near, jnp.max(s_new, axis=1, keepdims=True))
    p_new = jnp.where(live_new, jnp.exp(s_new - peak_n), 0.0)
    keep = jnp.exp(peak_near - peak_n)
    total_n = keep * total_near + jnp.sum(p_new, axis=1, keepdims=True)
    o_near = keep * sum_near + own_head(dot(p_new.astype(BF16), fv), heads, in_head)

    from_all = pltpu.make_async_remote_copy(
        src_ref=pob.at[pl.ds(0, engines - 1)],
        dst_ref=pib.at[pl.ds(0, engines - 1)],
        send_sem=sem_p.at[0],
        recv_sem=sem_p.at[1],
        device_id=(me, z),
        device_id_type=MESH,
    )
    from_all.wait_recv()
    pin = pib[...].astype(F32)
    o_in = pin[:, :sh, :].reshape(pairs, HD)
    parts = pin[:, sh:, :].reshape(pairs, HD).astype(BF16)
    third = iota((HD, HD), 0)
    add_up = jnp.where((third == 0) | (third == 32) | (third == 64), 1.0, 0.0).astype(BF16)
    lse_in = dot(parts, add_up)
    eye = iota((inner, inner), 0) == iota((inner, inner), 1)
    peak_lane = jnp.sum(jnp.where(eye, peak_n, 0.0), axis=0, keepdims=True)
    top = jnp.maximum(
        jnp.max(jnp.where(pick, lse_in[:, :inner], NEG), axis=0, keepdims=True), peak_lane
    )
    top_pair = jnp.sum(jnp.where(pick, top, 0.0), axis=1, keepdims=True)
    top_in = jnp.sum(jnp.where(eye, top, 0.0), axis=1, keepdims=True)
    valid = row_col > 0.0
    w_in = jnp.where(valid, jnp.exp(jnp.where(valid, lse_in - top_pair, 0.0)), 0.0)
    weighted = jnp.concatenate(
        [jnp.where(valid, w_in * o_in, 0.0), w_in], axis=1
    )
    first = weighted.astype(BF16)
    second = (weighted - first.astype(F32)).astype(BF16)
    collect = jnp.where(pick_t, 1.0, 0.0).astype(BF16)
    gathered = dot(collect, first) + dot(collect, second)
    w_near = jnp.exp(peak_n - top_in)
    result = (w_near * o_near + gathered[:, :HD]) / (w_near * total_n + gathered[:, HD:])
    for t in range(steps):
        for h in range(heads):
            j = t * heads + h
            out_v[t, :, h * HD : (h + 1) * HD] = result[j * rows : (j + 1) * rows, :].astype(BF16)

    everyone.wait_send()
    fresh_all.wait_send()
    from_all.wait_send()


def per_device(
    engines,
    tps,
    outgoing,
    span_target,
    span_row,
    span_block,
    span_tokens,
    norm_gain,
    key_weight,
    value_weight,
    fresh_states,
    queries,
    res_keys,
    res_values,
    res_len,
):
    sends, span, depth = outgoing.shape
    width = key_weight.shape[1]
    steps, rows, _ = queries.shape
    resident = res_keys.shape[1]
    heads = width // HD
    sh = steps * heads
    tokens = sends * span
    vmem = pl.BlockSpec(memory_space=pltpu.VMEM)
    hbm = pl.BlockSpec(memory_space=pltpu.HBM)
    chunks = len(chunk_bounds(depth))
    table = jnp.asarray(rope_tables(steps))
    return pl.pallas_call(
        functools.partial(kernel, engines, tps, sends, rows, steps),
        out_shape=jax.ShapeDtypeStruct((steps, rows, width), BF16),
        in_specs=[hbm] * 14,
        out_specs=vmem,
        scratch_shapes=[
            pltpu.VMEM((tokens, depth), BF16),
            pltpu.VMEM((tokens, depth), BF16),
            pltpu.VMEM((depth, width), BF16),
            pltpu.VMEM((depth, width), BF16),
            pltpu.VMEM((rows * resident, width), BF16),
            pltpu.VMEM((rows * resident, width), BF16),
            pltpu.VMEM((tokens, width), F32),
            pltpu.VMEM((tokens, width), F32),
            pltpu.VMEM((tokens, width), BF16),
            pltpu.VMEM((tokens, width), BF16),
            pltpu.VMEM((tokens, HD), F32),
            pltpu.VMEM((tokens, HD), F32),
            pltpu.VMEM((tokens, HD), F32),
            pltpu.VMEM((steps * 8, depth // 8), F32),
            pltpu.VMEM((steps * 8, depth // 8), BF16),
            pltpu.VMEM((tps, steps * 8, depth // 8), BF16),
            pltpu.VMEM((engines, sh, HD), F32),
            pltpu.VMEM((engines, sh, HD), F32),
            pltpu.VMEM((engines, 2 * sh, HD), BF16),
            pltpu.VMEM((engines, 2 * sh, HD), BF16),
            pltpu.VMEM((engines * sh, sends * sh), BF16),
            pltpu.SMEM((sends, engines), jnp.int32),
            pltpu.SMEM((sends, engines), jnp.int32),
            pltpu.SMEM((sends, engines), jnp.int32),
            pltpu.SMEM((rows,), jnp.int32),
            pltpu.VMEM((sends, engines), jnp.int32),
            pltpu.VMEM((sends, engines), jnp.int32),
            pltpu.VMEM((depth // HD, HD), F32),
            pltpu.VMEM(table.shape, F32),
            pltpu.VMEM((steps, depth), BF16),
            pltpu.VMEM((steps, rows, width), BF16),
            pltpu.SemaphoreType.DMA((chunks,)),
            pltpu.SemaphoreType.DMA((2, chunks)),
            pltpu.SemaphoreType.DMA((2,)),
            pltpu.SemaphoreType.DMA((10,)),
            pltpu.SemaphoreType.REGULAR,
            pltpu.SemaphoreType.DMA((2,)),
            pltpu.SemaphoreType.DMA((2,)),
            pltpu.SemaphoreType.DMA((2,)),
        ],
        compiler_params=pltpu.CompilerParams(
            collective_id=0, has_side_effects=True, vmem_limit_bytes=60 * 1024 * 1024
        ),
    )(
        outgoing.reshape(tokens, depth),
        span_target.T,
        span_row.T,
        span_block.T,
        span_tokens.T,
        res_len,
        norm_gain.reshape(depth // HD, HD),
        table,
        fresh_states.reshape(steps, depth),
        queries,
        key_weight,
        value_weight,
        res_keys.reshape(rows * resident, width),
        res_values.reshape(rows * resident, width),
    )


def solution(mesh):
    in_specs = (
        P("engine", None, None),
        P(),
        P(),
        P(),
        P(),
        P(),
        P(None, "tp"),
        P(None, "tp"),
        P(None, ("engine", "tp"), None),
        P(None, "engine", "tp"),
        P("engine", None, "tp"),
        P("engine", None, "tp"),
        P("engine"),
    )
    return jax.shard_map(
        functools.partial(per_device, mesh.shape["engine"], mesh.shape["tp"]),
        mesh=mesh,
        in_specs=in_specs,
        out_specs=P(None, "engine", "tp"),
        check_vma=False,
    )
```

```python
import functools
import math

import jax
import jax.numpy as jnp
import numpy as np
from jax import lax
from jax.experimental import pallas as pl
from jax.experimental.pallas import tpu as pltpu
from jax.sharding import PartitionSpec as P

MESH = pl.DeviceIdType.MESH
F32 = jnp.float32
BF16 = jnp.bfloat16
HD = 128
HALF = HD // 2
CTX = 2048
SPAN = 32
ROPE_BASE = 1000000.0
NORM_EPS = 1e-06
NEG = -1e30


def iota(shape, axis):
    return lax.broadcasted_iota(jnp.int32, shape, axis)


def rope_tables(steps):
    frequency = ROPE_BASE ** (-2.0 * np.arange(HALF) / HD)
    blocks = np.arange(CTX // SPAN + 8)[:, None] * SPAN * frequency[None, :]
    tokens = np.arange(SPAN)[:, None] * frequency[None, :]

    def wide(angles):
        cosine, sine = np.cos(angles), np.sin(angles)
        return np.concatenate([cosine, cosine], 1), np.concatenate([-sine, sine], 1)

    return np.concatenate([*wide(blocks), *wide(tokens)], 0).astype(np.float32)


def chunk_bounds(depth):
    edges = [depth * eighths // 8 for eighths in (0, 1, 3, 5, 7, 8)]
    return list(zip(edges[:-1], edges[1:], strict=True))


def far_first(engines):
    side = max(1, round(math.sqrt(engines // 2)))
    if side * side * 2 != engines:
        return [(0, 0, 0, i) for i in range(1, engines)]
    steps = [(x, y, c) for x in range(side) for y in range(side) for c in range(2)][1:]
    hops = lambda p: 2 * (min(p[0], side - p[0]) + min(p[1], side - p[1])) + p[2]
    return [(side, *p) for p in sorted(steps, key=hops, reverse=True)]


def dot(a, b):
    return jnp.dot(a, b, preferred_element_type=F32)


def dot_nt(a, b):
    return lax.dot_general(a, b, (((1,), (1,)), ((), ())), preferred_element_type=F32)


def per_head(x, count):
    return [x[:, h * HD : (h + 1) * HD] for h in range(count)]


def own_head(x, heads, head_of_row):
    blocks = per_head(x, heads)
    out = blocks[0]
    for h in range(1, heads):
        out = jnp.where(head_of_row == h, blocks[h], out)
    return out


def spread_heads(x, heads, head_of_row):
    return jnp.concatenate(
        [jnp.where(head_of_row == h, x, 0.0) for h in range(heads)], axis=1
    )


def kernel(
    engines,
    tps,
    sends,
    rows,
    steps,
    x_hbm,
    tgt_hbm,
    row_hbm,
    blk_hbm,
    tok_hbm,
    len_hbm,
    gain_hbm,
    tab_hbm,
    fresh_hbm,
    q_hbm,
    wk_hbm,
    wv_hbm,
    rk_hbm,
    rv_hbm,
    out_v,
    xv,
    nv,
    wk,
    wv,
    rk,
    rv,
    ak,
    av,
    kb,
    vb,
    squares,
    cosv,
    sinv,
    fst32,
    fst,
    fin,
    qob,
    qib,
    pob,
    pib,
    place,
    collect_v,
    add_v,
    tgt_s,
    blk_s,
    tok_s,
    len_s,
    tgt_v,
    row_v,
    gain_v,
    tab_v,
    fresh_v,
    q_v,
    sem_x,
    sem_w,
    sem_r,
    sem_s,
    here,
    sem_f,
    sem_q,
    sem_p,
):
    me = lax.axis_index("engine")
    z = lax.axis_index("tp")
    order = far_first(engines)

    def partner(step):
        side, dx, dy, dc = step
        if side == 0:
            return lax.rem(me + dc, engines)
        x, y, core = me // (2 * side), me // 2 % side, me % 2
        return (lax.rem(x + dx, side) * side + lax.rem(y + dy, side)) * 2 + lax.rem(core + dc, 2)

    width = wk.shape[1]
    depth = wk.shape[0]
    heads = width // HD
    sh = steps * heads
    pairs = engines * sh
    inner = sh * rows
    tokens = sends * SPAN
    bounds = chunk_bounds(depth)
    chunks = len(bounds)

    def x_copy(c):
        part = pl.ds(bounds[c][0], bounds[c][1] - bounds[c][0])
        return pltpu.make_async_copy(x_hbm.at[:, part], xv.at[:, part], sem_x.at[c])

    def w_copy(m, c):
        part = pl.ds(bounds[c][0], bounds[c][1] - bounds[c][0])
        source, target = ((wk_hbm, wk), (wv_hbm, wv))[m]
        return pltpu.make_async_copy(source.at[part], target.at[part], sem_w.at[m, c])

    barrier = pltpu.get_barrier_semaphore()
    for step in order:
        pl.semaphore_signal(
            barrier, inc=1, device_id=(partner(step), z), device_id_type=MESH
        )

    def greet_higher(other, carry):
        pl.semaphore_signal(barrier, inc=1, device_id=(me, other), device_id_type=MESH)
        return carry

    lax.fori_loop(z + 1, tps, greet_higher, 0)

    small = [
        pltpu.make_async_copy(source, target, sem_s.at[i])
        for i, (source, target) in enumerate(
            (
                (q_hbm, q_v),
                (tgt_hbm, tgt_v),
                (row_hbm, row_v),
                (gain_hbm, gain_v),
                (fresh_hbm, fresh_v),
                (tgt_hbm, tgt_s),
                (blk_hbm, blk_s),
                (tok_hbm, tok_s),
                (tab_hbm, tab_v),
                (len_hbm, len_s),
            )
        )
    ]
    for copy in small:
        copy.start()

    def start_chunk(c):
        x_copy(c).start()
        w_copy(0, c).start()
        w_copy(1, c).start()

    start_chunk(0)

    def turn(raw, cosine, sine):
        return raw * cosine + pltpu.roll(raw, HALF, 1) * sine

    def prepare(c):
        for j in range(bounds[c][0] // HD, bounds[c][1] // HD):
            lanes = slice(j * HD, (j + 1) * HD)
            block = xv[:, lanes].astype(F32)
            nv[:, lanes] = (block * gain_v[j : j + 1, :]).astype(BF16)
            square = block * block
            folded = square if j == bounds[c][0] // HD else folded + square
        squares[...] = folded if c == 0 else squares[...] + folded

    def multiply(c):
        part = slice(*bounds[c])
        for weight, total in ((wk, ak), (wv, av)):
            raw = dot(nv[:, part], weight[part, :])
            total[...] = raw if c == 0 else total[...] + raw

    def wait_chunk(c):
        x_copy(c).wait()
        w_copy(0, c).wait()
        w_copy(1, c).wait()

    for copy in small[:3]:
        copy.wait()
    q = q_v[...].astype(F32)
    q64 = jnp.concatenate(
        [q[s][:, h * HD : (h + 1) * HD] for s in range(steps) for h in range(heads)], axis=0
    )
    hit = tgt_v[...] == me
    arrives = jnp.sum(jnp.where(hit, (row_v[...] + 1).astype(F32), 0.0), axis=0, keepdims=True)
    pe = iota((pairs, engines), 0) // sh
    row_col = jnp.sum(
        jnp.where(pe == iota((pairs, engines), 1), arrives, 0.0), axis=1, keepdims=True
    )
    arr_col = jnp.sum(
        jnp.where(
            iota((engines, engines), 0) == iota((engines, engines), 1), arrives, 0.0
        ),
        axis=1,
        keepdims=True,
    )
    row_lane = jnp.sum(
        jnp.where(
            iota((engines, pairs), 0) == iota((engines, pairs), 1) // sh, arr_col, 0.0
        ),
        axis=0,
        keepdims=True,
    )
    gi, gl = iota((pairs, inner), 0), iota((pairs, inner), 1)
    pick = (row_col == (gl % rows + 1).astype(F32)) & (gi % sh == gl // rows)
    ti, tl = iota((inner, pairs), 0), iota((inner, pairs), 1)
    pick_t = (row_lane == (ti % rows + 1).astype(F32)) & (tl % sh == ti // rows)
    qout = dot(jnp.where(pick, 1.0, 0.0).astype(BF16), q64.astype(BF16))
    qob[...] = qout.reshape(engines, sh, HD).astype(BF16)
    qib[me] = jnp.zeros((sh, HD), BF16)


    def q_copy(step):
        other = partner(step)
        return pltpu.make_async_remote_copy(
            src_ref=qob.at[other],
            dst_ref=qib.at[me],
            send_sem=sem_q.at[0],
            recv_sem=sem_q.at[1],
            device_id=(other, z),
            device_id_type=MESH,
        )

    for c in range(1, chunks):
        start_chunk(c)
    rk_copy = pltpu.make_async_copy(rk_hbm, rk, sem_r.at[0])
    rv_copy = pltpu.make_async_copy(rv_hbm, rv, sem_r.at[1])
    rk_copy.start()
    rv_copy.start()


    small[3].wait()
    wait_chunk(0)
    prepare(0)
    multiply(0)

    for copy in small[4:]:
        copy.wait()

    fw = depth // 8
    fresh = fresh_v[...].astype(F32)
    fresh = fresh * lax.rsqrt(jnp.mean(fresh * fresh, axis=1, keepdims=True) + NORM_EPS)
    for s in range(steps):
        for j in range(depth // HD):
            row, at = s * 8 + j * HD // fw, j * HD % fw
            fst32[row : row + 1, at : at + HD] = (
                fresh[s : s + 1, j * HD : (j + 1) * HD] * gain_v[j : j + 1, :]
            )
    fst[...] = fst32[...].astype(BF16)
    fin[z] = fst[...]


    def f_copy(other):
        return pltpu.make_async_remote_copy(
            src_ref=fst,
            dst_ref=fin.at[z],
            send_sem=sem_f.at[0],
            recv_sem=sem_f.at[1],
            device_id=(me, other),
            device_id_type=MESH,
        )

    def answer_lower(other, carry):
        pl.semaphore_signal(here, inc=1, device_id=(me, other), device_id_type=MESH)
        f_copy(other).start()
        return carry

    def send_higher(other, carry):
        f_copy(other).start()
        return carry

    pl.semaphore_wait(barrier, engines - 1 + z)
    lax.fori_loop(0, z, answer_lower, 0)
    for step in order:
        q_copy(step).start()

    wait_chunk(1)
    prepare(1)
    multiply(1)

    nb = CTX // SPAN + 8
    tok_cos = tab_v[2 * nb : 2 * nb + SPAN, :]
    tok_sin = tab_v[2 * nb + SPAN : 2 * nb + 2 * SPAN, :]
    span_lane = iota((1, sends * sh), 1)
    lane_target = jnp.full((1, sends * sh), -1, jnp.int32)
    for k in range(sends):
        b = blk_s[k, me]
        block_cos = tab_v[pl.ds(b, 1), :]
        block_sin = tab_v[pl.ds(b + nb, 1), :]
        cosv[k * SPAN : (k + 1) * SPAN, :] = block_cos * tok_cos - block_sin * tok_sin
        sinv[k * SPAN : (k + 1) * SPAN, :] = block_sin * tok_cos + block_cos * tok_sin
        lane_target = jnp.where(span_lane // sh == k, tgt_s[k, me], lane_target)
    oi, ol = iota((pairs, sends * sh), 0), iota((pairs, sends * sh), 1)
    place[...] = jnp.where((lane_target == oi // sh) & (oi % sh == ol % sh), 1.0, 0.0).astype(BF16)

    for c in range(2, chunks):
        wait_chunk(c)
        prepare(c)
        multiply(c)
    mean = jnp.sum(squares[...], axis=1, keepdims=True) * (1.0 / depth)
    factor = lax.rsqrt(mean + NORM_EPS)
    cosine = cosv[...] * factor
    sine = sinv[...] * factor
    for h in range(heads):
        head = slice(h * HD, (h + 1) * HD)
        kb[:, head] = turn(ak[:, head], cosine, sine).astype(BF16)

    scale = 1.0 / math.sqrt(HD)
    everyone = pltpu.make_async_remote_copy(
        src_ref=qob.at[pl.ds(0, engines - 1)],
        dst_ref=qib.at[pl.ds(0, engines - 1)],
        send_sem=sem_q.at[0],
        recv_sem=sem_q.at[1],
        device_id=(me, z),
        device_id_type=MESH,
    )

    def reach_higher():
        @pl.when(z < tps - 1)
        def _():
            pl.semaphore_wait(here, tps - 1 - z)

        lax.fori_loop(z + 1, tps, send_higher, 0)

    @pl.when(z >= tps // 2)
    def _():
        reach_higher()

    everyone.wait_recv()
    vb[...] = (av[...] * factor).astype(BF16)
    made = []
    for g in range(0, sends, HD // SPAN):
        spans = range(g, min(g + HD // SPAN, sends))
        count = len(spans)
        group = slice(g * SPAN, (g + count) * SPAN)
        q_g = jnp.concatenate([qib[tgt_s[k, me]].astype(F32) for k in spans], axis=0)
        g_row = iota((count * sh, 1), 0)
        g_lane = iota((1, count * SPAN), 1)
        edge = jnp.zeros((count * sh, 1), jnp.int32)
        for j, k in enumerate(spans):
            edge = jnp.where(g_row // sh == j, j * SPAN + tok_s[k, me], edge)
        live = (g_lane >= g_row // sh * SPAN) & (g_lane < edge)
        s = dot_nt(spread_heads(q_g, heads, g_row % heads).astype(BF16), kb[group, :]) * scale
        s = jnp.where(live, s, NEG)
        peak = jnp.max(s, axis=1, keepdims=True)
        p = jnp.where(live, jnp.exp(s - peak), 0.0)
        total = jnp.sum(p, axis=1, keepdims=True)
        o = own_head(dot(p.astype(BF16), vb[group, :]), heads, g_row % heads) / total
        lse = peak + jnp.log(total)
        hi = lse.astype(BF16).astype(F32)
        mid = (lse - hi).astype(BF16).astype(F32)
        low = lse - hi - mid
        lane = iota((count * sh, HD), 1)
        coded = jnp.where(lane < 32, hi, jnp.where(lane < 64, mid, low))
        made.append(jnp.concatenate([o, coded], axis=1).astype(BF16))
    placed = dot(place[...], jnp.concatenate(made, axis=0))
    pob[...] = jnp.concatenate(
        [placed[:, :HD].reshape(engines, sh, HD), placed[:, HD:].reshape(engines, sh, HD)], axis=1
    ).astype(BF16)

    def p_copy(step):
        other = partner(step)
        return pltpu.make_async_remote_copy(
            src_ref=pob.at[other],
            dst_ref=pib.at[me],
            send_sem=sem_p.at[0],
            recv_sem=sem_p.at[1],
            device_id=(other, z),
            device_id_type=MESH,
        )

    for step in order:
        p_copy(step).start()
    pib[me] = jnp.zeros((2 * sh, HD), BF16)

    @pl.when(z < tps // 2)
    def _():
        reach_higher()

    near = rk.shape[0]
    resident = near // rows
    rk_copy.wait()
    rv_copy.wait()
    in_row = iota((inner, 1), 0)
    in_head = in_row // rows % heads
    q_near = spread_heads(q64, heads, in_head).astype(BF16)
    lane_near = iota((1, near), 1)
    col_row = jnp.full((1, near), -1, jnp.int32)
    for r in range(rows):
        ok = (lane_near >= r * resident) & (lane_near < r * resident + len_s[r])
        col_row = jnp.where(ok, r, col_row)
    live_near = col_row == in_row % rows
    s_near = jnp.where(live_near, dot_nt(q_near, rk[...]) * scale, NEG)
    peak_near = jnp.max(s_near, axis=1, keepdims=True)
    p_near = jnp.where(live_near, jnp.exp(s_near - peak_near), 0.0)
    total_near = jnp.sum(p_near, axis=1, keepdims=True)
    sum_near = own_head(dot(p_near.astype(BF16), rv[...]), heads, in_head)

    fresh_all = pltpu.make_async_remote_copy(
        src_ref=fin.at[pl.ds(0, tps - 1)],
        dst_ref=fin.at[pl.ds(0, tps - 1)],
        send_sem=sem_f.at[0],
        recv_sem=sem_f.at[1],
        device_id=(me, z),
        device_id_type=MESH,
    )
    fresh_all.wait_recv()
    fr = rows * steps * 8
    ri, rl = iota((fr, fr), 0), iota((fr, fr), 1)
    want = (ri % rows) * (steps * 8) + (ri // rows % steps) * 8 + ri // (rows * steps)
    order = jnp.where(rl == want, 1.0, 0.0).astype(BF16)
    sorted_fresh = dot(order, fin[...].reshape(fr, fw)).astype(BF16)
    new = rows * steps
    fn = jnp.concatenate(
        [sorted_fresh[c * new : (c + 1) * new, :] for c in range(8)], axis=1
    )
    f_step = iota((new, 1), 0) // rows
    f_cos = jnp.zeros((new, HD), F32)
    f_sin = jnp.zeros((new, HD), F32)
    bc = CTX // SPAN
    for t in range(steps):
        c0, s0 = tab_v[bc : bc + 1, :], tab_v[nb + bc : nb + bc + 1, :]
        c1, s1 = tok_cos[t : t + 1, :], tok_sin[t : t + 1, :]
        f_cos = jnp.where(f_step == t, c0 * c1 - s0 * s1, f_cos)
        f_sin = jnp.where(f_step == t, s0 * c1 + c0 * s1, f_sin)
    raw = dot(fn, wk[...])
    fk = jnp.concatenate([turn(b, f_cos, f_sin) for b in per_head(raw, heads)], axis=1).astype(BF16)
    fv = dot(fn, wv[...]).astype(BF16)

    lane_new = iota((1, new), 1)
    live_new = (lane_new % rows == in_row % rows) & (lane_new // rows <= in_row // (rows * heads))
    s_new = jnp.where(live_new, dot_nt(q_near, fk) * scale, NEG)
    peak_n = jnp.maximum(peak_near, jnp.max(s_new, axis=1, keepdims=True))
    p_new = jnp.where(live_new, jnp.exp(s_new - peak_n), 0.0)
    keep = jnp.exp(peak_near - peak_n)
    total_n = keep * total_near + jnp.sum(p_new, axis=1, keepdims=True)
    o_near = keep * sum_near + own_head(dot(p_new.astype(BF16), fv), heads, in_head)

    third = iota((HD, HD), 0)
    add_up = jnp.where((third == 0) | (third == 32) | (third == 64), 1.0, 0.0).astype(BF16)
    eye = iota((inner, inner), 0) == iota((inner, inner), 1)
    peak_lane = jnp.sum(jnp.where(eye, peak_n, 0.0), axis=0, keepdims=True)
    collect_v[...] = jnp.where(pick_t, 1.0, 0.0).astype(BF16)
    add_v[...] = add_up
    from_all = pltpu.make_async_remote_copy(
        src_ref=pob.at[pl.ds(0, engines - 1)],
        dst_ref=pib.at[pl.ds(0, engines - 1)],
        send_sem=sem_p.at[0],
        recv_sem=sem_p.at[1],
        device_id=(me, z),
        device_id_type=MESH,
    )
    from_all.wait_recv()
    pin = pib[...].astype(F32)
    o_in = pin[:, :sh, :].reshape(pairs, HD)
    parts = pin[:, sh:, :].reshape(pairs, HD).astype(BF16)
    lse_in = dot(parts, add_v[...])
    top = jnp.maximum(
        jnp.max(jnp.where(pick, lse_in[:, :inner], NEG), axis=0, keepdims=True), peak_lane
    )
    top_pair = jnp.sum(jnp.where(pick, top, 0.0), axis=1, keepdims=True)
    top_in = jnp.sum(jnp.where(eye, top, 0.0), axis=1, keepdims=True)
    valid = row_col > 0.0
    w_in = jnp.where(valid, jnp.exp(jnp.where(valid, lse_in - top_pair, 0.0)), 0.0)
    weighted = jnp.concatenate(
        [jnp.where(valid, w_in * o_in, 0.0), w_in], axis=1
    )
    first = weighted.astype(BF16)
    second = (weighted - first.astype(F32)).astype(BF16)
    gathered = dot(collect_v[...], first) + dot(collect_v[...], second)
    w_near = jnp.exp(peak_n - top_in)
    result = (w_near * o_near + gathered[:, :HD]) / (w_near * total_n + gathered[:, HD:])
    for t in range(steps):
        for h in range(heads):
            j = t * heads + h
            out_v[t, :, h * HD : (h + 1) * HD] = result[j * rows : (j + 1) * rows, :].astype(BF16)

    everyone.wait_send()
    fresh_all.wait_send()
    from_all.wait_send()


def per_device(
    engines,
    tps,
    outgoing,
    span_target,
    span_row,
    span_block,
    span_tokens,
    norm_gain,
    key_weight,
    value_weight,
    fresh_states,
    queries,
    res_keys,
    res_values,
    res_len,
):
    sends, span, depth = outgoing.shape
    width = key_weight.shape[1]
    steps, rows, _ = queries.shape
    resident = res_keys.shape[1]
    heads = width // HD
    sh = steps * heads
    tokens = sends * span
    vmem = pl.BlockSpec(memory_space=pltpu.VMEM)
    hbm = pl.BlockSpec(memory_space=pltpu.HBM)
    chunks = len(chunk_bounds(depth))
    table = jnp.asarray(rope_tables(steps))
    return pl.pallas_call(
        functools.partial(kernel, engines, tps, sends, rows, steps),
        out_shape=jax.ShapeDtypeStruct((steps, rows, width), BF16),
        in_specs=[hbm] * 14,
        out_specs=vmem,
        scratch_shapes=[
            pltpu.VMEM((tokens, depth), BF16),
            pltpu.VMEM((tokens, depth), BF16),
            pltpu.VMEM((depth, width), BF16),
            pltpu.VMEM((depth, width), BF16),
            pltpu.VMEM((rows * resident, width), BF16),
            pltpu.VMEM((rows * resident, width), BF16),
            pltpu.VMEM((tokens, width), F32),
            pltpu.VMEM((tokens, width), F32),
            pltpu.VMEM((tokens, width), BF16),
            pltpu.VMEM((tokens, width), BF16),
            pltpu.VMEM((tokens, HD), F32),
            pltpu.VMEM((tokens, HD), F32),
            pltpu.VMEM((tokens, HD), F32),
            pltpu.VMEM((steps * 8, depth // 8), F32),
            pltpu.VMEM((steps * 8, depth // 8), BF16),
            pltpu.VMEM((tps, steps * 8, depth // 8), BF16),
            pltpu.VMEM((engines, sh, HD), BF16),
            pltpu.VMEM((engines, sh, HD), BF16),
            pltpu.VMEM((engines, 2 * sh, HD), BF16),
            pltpu.VMEM((engines, 2 * sh, HD), BF16),
            pltpu.VMEM((engines * sh, sends * sh), BF16),
            pltpu.VMEM((sh * rows, engines * sh), BF16),
            pltpu.VMEM((HD, HD), BF16),
            pltpu.SMEM((sends, engines), jnp.int32),
            pltpu.SMEM((sends, engines), jnp.int32),
            pltpu.SMEM((sends, engines), jnp.int32),
            pltpu.SMEM((rows,), jnp.int32),
            pltpu.VMEM((sends, engines), jnp.int32),
            pltpu.VMEM((sends, engines), jnp.int32),
            pltpu.VMEM((depth // HD, HD), F32),
            pltpu.VMEM(table.shape, F32),
            pltpu.VMEM((steps, depth), BF16),
            pltpu.VMEM((steps, rows, width), BF16),
            pltpu.SemaphoreType.DMA((chunks,)),
            pltpu.SemaphoreType.DMA((2, chunks)),
            pltpu.SemaphoreType.DMA((2,)),
            pltpu.SemaphoreType.DMA((10,)),
            pltpu.SemaphoreType.REGULAR,
            pltpu.SemaphoreType.DMA((2,)),
            pltpu.SemaphoreType.DMA((2,)),
            pltpu.SemaphoreType.DMA((2,)),
        ],
        compiler_params=pltpu.CompilerParams(
            collective_id=0, has_side_effects=True, vmem_limit_bytes=60 * 1024 * 1024
        ),
    )(
        outgoing.reshape(tokens, depth),
        span_target.T,
        span_row.T,
        span_block.T,
        span_tokens.T,
        res_len,
        norm_gain.reshape(depth // HD, HD),
        table,
        fresh_states.reshape(steps, depth),
        queries,
        key_weight,
        value_weight,
        res_keys.reshape(rows * resident, width),
        res_values.reshape(rows * resident, width),
    )


def solution(mesh):
    in_specs = (
        P("engine", None, None),
        P(),
        P(),
        P(),
        P(),
        P(),
        P(None, "tp"),
        P(None, "tp"),
        P(None, ("engine", "tp"), None),
        P(None, "engine", "tp"),
        P("engine", None, "tp"),
        P("engine", None, "tp"),
        P("engine"),
    )
    return jax.shard_map(
        functools.partial(per_device, mesh.shape["engine"], mesh.shape["tp"]),
        mesh=mesh,
        in_specs=in_specs,
        out_specs=P(None, "engine", "tp"),
        check_vma=False,
    )
```

```python
import functools
import math

import jax
import jax.numpy as jnp
import numpy as np
from jax import lax
from jax.experimental import pallas as pl
from jax.experimental.pallas import tpu as pltpu
from jax.sharding import PartitionSpec as P

MESH = pl.DeviceIdType.MESH
F32 = jnp.float32
BF16 = jnp.bfloat16
HD = 128
HALF = HD // 2
CTX = 2048
SPAN = 32
ROPE_BASE = 1000000.0
NORM_EPS = 1e-06
NEG = -1e30


def iota(shape, axis):
    return lax.broadcasted_iota(jnp.int32, shape, axis)


def rope_tables(steps):
    frequency = ROPE_BASE ** (-2.0 * np.arange(HALF) / HD)
    blocks = np.arange(CTX // SPAN + 8)[:, None] * SPAN * frequency[None, :]
    tokens = np.arange(SPAN)[:, None] * frequency[None, :]

    def wide(angles):
        cosine, sine = np.cos(angles), np.sin(angles)
        return np.concatenate([cosine, cosine], 1), np.concatenate([-sine, sine], 1)

    return np.concatenate([*wide(blocks), *wide(tokens)], 0).astype(np.float32)


def chunk_bounds(depth):
    edges = [depth * eighths // 8 for eighths in (0, 1, 4, 7, 8)]
    return list(zip(edges[:-1], edges[1:], strict=True))


def far_first(engines):
    side = max(1, round(math.sqrt(engines // 2)))
    if side * side * 2 != engines:
        return [(0, 0, 0, i) for i in range(1, engines)]
    steps = [(x, y, c) for x in range(side) for y in range(side) for c in range(2)][1:]
    hops = lambda p: 2 * (min(p[0], side - p[0]) + min(p[1], side - p[1])) + p[2]
    return [(side, *p) for p in sorted(steps, key=hops, reverse=True)]


def dot(a, b):
    return jnp.dot(a, b, preferred_element_type=F32)


def dot_nt(a, b):
    return lax.dot_general(a, b, (((1,), (1,)), ((), ())), preferred_element_type=F32)


def per_head(x, count):
    return [x[:, h * HD : (h + 1) * HD] for h in range(count)]


def own_head(x, heads, head_of_row):
    blocks = per_head(x, heads)
    out = blocks[0]
    for h in range(1, heads):
        out = jnp.where(head_of_row == h, blocks[h], out)
    return out


def spread_heads(x, heads, head_of_row):
    return jnp.concatenate(
        [jnp.where(head_of_row == h, x, 0.0) for h in range(heads)], axis=1
    )


def kernel(
    engines,
    tps,
    sends,
    rows,
    steps,
    x_hbm,
    tgt_hbm,
    row_hbm,
    blk_hbm,
    tok_hbm,
    len_hbm,
    gain_hbm,
    tab_hbm,
    fresh_hbm,
    q_hbm,
    wk_hbm,
    wv_hbm,
    rk_hbm,
    rv_hbm,
    out_v,
    xv,
    nv,
    wk,
    wv,
    rk,
    rv,
    ak,
    av,
    kb,
    vb,
    squares,
    cosv,
    sinv,
    fst32,
    fst,
    fin,
    qob,
    qib,
    pob,
    pib,
    place,
    collect_v,
    add_v,
    tgt_s,
    blk_s,
    tok_s,
    len_s,
    tgt_v,
    row_v,
    gain_v,
    tab_v,
    fresh_v,
    q_v,
    sem_x,
    sem_w,
    sem_r,
    sem_s,
    here,
    sem_f,
    sem_q,
    sem_p,
):
    me = lax.axis_index("engine")
    z = lax.axis_index("tp")
    order = far_first(engines)

    side = order[0][0]
    if side:
        at_x = [lax.rem(me // (2 * side) + d, side) * (2 * side) for d in range(side)]
        at_y = [lax.rem(me // 2 % side + d, side) * 2 for d in range(side)]
        at_core = [lax.rem(me % 2 + d, 2) for d in range(2)]

    def partner(step):
        if side == 0:
            return lax.rem(me + step[3], engines)
        return at_x[step[1]] + at_y[step[2]] + at_core[step[3]]

    width = wk.shape[1]
    depth = wk.shape[0]
    heads = width // HD
    sh = steps * heads
    pairs = engines * sh
    inner = sh * rows
    tokens = sends * SPAN
    bounds = chunk_bounds(depth)
    chunks = len(bounds)

    def x_copy(c):
        part = pl.ds(bounds[c][0], bounds[c][1] - bounds[c][0])
        return pltpu.make_async_copy(x_hbm.at[:, part], xv.at[:, part], sem_x.at[c])

    def w_copy(m, c):
        part = pl.ds(bounds[c][0], bounds[c][1] - bounds[c][0])
        source, target = ((wk_hbm, wk), (wv_hbm, wv))[m]
        return pltpu.make_async_copy(source.at[part], target.at[part], sem_w.at[m, c])

    small = [
        pltpu.make_async_copy(source, target, sem_s.at[i])
        for i, (source, target) in enumerate(
            (
                (q_hbm, q_v),
                (tgt_hbm, tgt_v),
                (row_hbm, row_v),
                (gain_hbm, gain_v),
                (fresh_hbm, fresh_v),
                (tgt_hbm, tgt_s),
                (blk_hbm, blk_s),
                (tok_hbm, tok_s),
                (tab_hbm, tab_v),
                (len_hbm, len_s),
            )
        )
    ]

    def start_chunk(c):
        x_copy(c).start()
        w_copy(0, c).start()
        w_copy(1, c).start()


    for copy in small[:4]:
        copy.start()
    start_chunk(0)

    barrier = pltpu.get_barrier_semaphore()
    for step in order:
        pl.semaphore_signal(
            barrier, inc=1, device_id=(partner(step), z), device_id_type=MESH
        )

    def greet_higher(other, carry):
        pl.semaphore_signal(barrier, inc=1, device_id=(me, other), device_id_type=MESH)
        return carry

    lax.fori_loop(z + 1, tps, greet_higher, 0)

    for copy in small[4:]:
        copy.start()

    def turn(raw, cosine, sine):
        return raw * cosine + pltpu.roll(raw, HALF, 1) * sine

    def prepare(c):
        for j in range(bounds[c][0] // HD, bounds[c][1] // HD):
            lanes = slice(j * HD, (j + 1) * HD)
            block = xv[:, lanes].astype(F32)
            nv[:, lanes] = (block * gain_v[j : j + 1, :]).astype(BF16)
            square = block * block
            folded = square if j == bounds[c][0] // HD else folded + square
        squares[...] = folded if c == 0 else squares[...] + folded

    def multiply(c):
        part = slice(*bounds[c])
        for weight, total in ((wk, ak), (wv, av)):
            raw = dot(nv[:, part], weight[part, :])
            total[...] = raw if c == 0 else total[...] + raw

    def wait_chunk(c):
        x_copy(c).wait()
        w_copy(0, c).wait()
        w_copy(1, c).wait()

    for copy in small[:3]:
        copy.wait()
    q = q_v[...].astype(F32)
    q64 = jnp.concatenate(
        [q[s][:, h * HD : (h + 1) * HD] for s in range(steps) for h in range(heads)], axis=0
    )
    hit = tgt_v[...] == me
    arrives = jnp.sum(jnp.where(hit, (row_v[...] + 1).astype(F32), 0.0), axis=0, keepdims=True)
    pe = iota((pairs, engines), 0) // sh
    row_col = jnp.sum(
        jnp.where(pe == iota((pairs, engines), 1), arrives, 0.0), axis=1, keepdims=True
    )
    arr_col = jnp.sum(
        jnp.where(
            iota((engines, engines), 0) == iota((engines, engines), 1), arrives, 0.0
        ),
        axis=1,
        keepdims=True,
    )
    row_lane = jnp.sum(
        jnp.where(
            iota((engines, pairs), 0) == iota((engines, pairs), 1) // sh, arr_col, 0.0
        ),
        axis=0,
        keepdims=True,
    )
    gi, gl = iota((pairs, inner), 0), iota((pairs, inner), 1)
    pick = (row_col == (gl % rows + 1).astype(F32)) & (gi % sh == gl // rows)
    ti, tl = iota((inner, pairs), 0), iota((inner, pairs), 1)
    pick_t = (row_lane == (ti % rows + 1).astype(F32)) & (tl % sh == ti // rows)
    qout = dot(jnp.where(pick, 1.0, 0.0).astype(BF16), q64.astype(BF16))
    qob[...] = qout.reshape(engines, sh, HD).astype(BF16)
    qib[me] = jnp.zeros((sh, HD), BF16)


    def q_copy(step):
        other = partner(step)
        return pltpu.make_async_remote_copy(
            src_ref=qob.at[other],
            dst_ref=qib.at[me],
            send_sem=sem_q.at[0],
            recv_sem=sem_q.at[1],
            device_id=(other, z),
            device_id_type=MESH,
        )

    for c in range(1, chunks):
        start_chunk(c)
    rk_copy = pltpu.make_async_copy(rk_hbm, rk, sem_r.at[0])
    rv_copy = pltpu.make_async_copy(rv_hbm, rv, sem_r.at[1])
    rk_copy.start()
    rv_copy.start()


    small[3].wait()
    wait_chunk(0)
    prepare(0)
    multiply(0)

    for copy in small[4:]:
        copy.wait()

    fw = depth // 8
    fresh = fresh_v[...].astype(F32)
    fresh = fresh * lax.rsqrt(jnp.mean(fresh * fresh, axis=1, keepdims=True) + NORM_EPS)
    for s in range(steps):
        for j in range(depth // HD):
            row, at = s * 8 + j * HD // fw, j * HD % fw
            fst32[row : row + 1, at : at + HD] = (
                fresh[s : s + 1, j * HD : (j + 1) * HD] * gain_v[j : j + 1, :]
            )
    fst[...] = fst32[...].astype(BF16)
    fin[z] = fst[...]


    def f_copy(other):
        return pltpu.make_async_remote_copy(
            src_ref=fst,
            dst_ref=fin.at[z],
            send_sem=sem_f.at[0],
            recv_sem=sem_f.at[1],
            device_id=(me, other),
            device_id_type=MESH,
        )

    def answer_lower(other, carry):
        pl.semaphore_signal(here, inc=1, device_id=(me, other), device_id_type=MESH)
        f_copy(other).start()
        return carry

    def send_higher(other, carry):
        f_copy(other).start()
        return carry

    pl.semaphore_wait(barrier, engines - 1 + z)
    lax.fori_loop(0, z, answer_lower, 0)
    for step in order:
        q_copy(step).start()

    wait_chunk(1)
    prepare(1)
    multiply(1)

    nb = CTX // SPAN + 8
    tok_cos = tab_v[2 * nb : 2 * nb + SPAN, :]
    tok_sin = tab_v[2 * nb + SPAN : 2 * nb + 2 * SPAN, :]
    span_lane = iota((1, sends * sh), 1)
    lane_target = jnp.full((1, sends * sh), -1, jnp.int32)
    for k in range(sends):
        b = blk_s[k, me]
        block_cos = tab_v[pl.ds(b, 1), :]
        block_sin = tab_v[pl.ds(b + nb, 1), :]
        cosv[k * SPAN : (k + 1) * SPAN, :] = block_cos * tok_cos - block_sin * tok_sin
        sinv[k * SPAN : (k + 1) * SPAN, :] = block_sin * tok_cos + block_cos * tok_sin
        lane_target = jnp.where(span_lane // sh == k, tgt_s[k, me], lane_target)
    oi, ol = iota((pairs, sends * sh), 0), iota((pairs, sends * sh), 1)
    place[...] = jnp.where((lane_target == oi // sh) & (oi % sh == ol % sh), 1.0, 0.0).astype(BF16)

    for c in range(2, chunks):
        wait_chunk(c)
        prepare(c)
        multiply(c)
    mean = jnp.sum(squares[...], axis=1, keepdims=True) * (1.0 / depth)
    factor = lax.rsqrt(mean + NORM_EPS)
    cosine = cosv[...] * factor
    sine = sinv[...] * factor
    for h in range(heads):
        head = slice(h * HD, (h + 1) * HD)
        kb[:, head] = turn(ak[:, head], cosine, sine).astype(BF16)

    scale = 1.0 / math.sqrt(HD)
    everyone = pltpu.make_async_remote_copy(
        src_ref=qob.at[pl.ds(0, engines - 1)],
        dst_ref=qib.at[pl.ds(0, engines - 1)],
        send_sem=sem_q.at[0],
        recv_sem=sem_q.at[1],
        device_id=(me, z),
        device_id_type=MESH,
    )

    def reach_higher():
        @pl.when(z < tps - 1)
        def _():
            pl.semaphore_wait(here, tps - 1 - z)

        lax.fori_loop(z + 1, tps, send_higher, 0)

    @pl.when(z >= tps // 2)
    def _():
        reach_higher()

    everyone.wait_recv()
    vb[...] = (av[...] * factor).astype(BF16)
    made = []
    for g in range(0, sends, HD // SPAN):
        spans = range(g, min(g + HD // SPAN, sends))
        count = len(spans)
        group = slice(g * SPAN, (g + count) * SPAN)
        q_g = jnp.concatenate([qib[tgt_s[k, me]].astype(F32) for k in spans], axis=0)
        g_row = iota((count * sh, 1), 0)
        g_lane = iota((1, count * SPAN), 1)
        edge = jnp.zeros((count * sh, 1), jnp.int32)
        for j, k in enumerate(spans):
            edge = jnp.where(g_row // sh == j, j * SPAN + tok_s[k, me], edge)
        live = (g_lane >= g_row // sh * SPAN) & (g_lane < edge)
        s = dot_nt(spread_heads(q_g, heads, g_row % heads).astype(BF16), kb[group, :]) * scale
        s = jnp.where(live, s, NEG)
        peak = jnp.max(s, axis=1, keepdims=True)
        p = jnp.where(live, jnp.exp(s - peak), 0.0)
        total = jnp.sum(p, axis=1, keepdims=True)
        o = own_head(dot(p.astype(BF16), vb[group, :]), heads, g_row % heads) / total
        lse = peak + jnp.log(total)
        hi = lse.astype(BF16).astype(F32)
        mid = (lse - hi).astype(BF16).astype(F32)
        low = lse - hi - mid
        lane = iota((count * sh, HD), 1)
        coded = jnp.where(lane < 32, hi, jnp.where(lane < 64, mid, low))
        made.append(jnp.concatenate([o, coded], axis=1).astype(BF16))
    placed = dot(place[...], jnp.concatenate(made, axis=0))
    pob[...] = jnp.concatenate(
        [placed[:, :HD].reshape(engines, sh, HD), placed[:, HD:].reshape(engines, sh, HD)], axis=1
    ).astype(BF16)

    def p_copy(step):
        other = partner(step)
        return pltpu.make_async_remote_copy(
            src_ref=pob.at[other],
            dst_ref=pib.at[me],
            send_sem=sem_p.at[0],
            recv_sem=sem_p.at[1],
            device_id=(other, z),
            device_id_type=MESH,
        )

    for step in order:
        p_copy(step).start()
    pib[me] = jnp.zeros((2 * sh, HD), BF16)

    @pl.when(z < tps // 2)
    def _():
        reach_higher()

    near = rk.shape[0]
    resident = near // rows
    rk_copy.wait()
    rv_copy.wait()
    in_row = iota((inner, 1), 0)
    in_head = in_row // rows % heads
    q_near = spread_heads(q64, heads, in_head).astype(BF16)
    lane_near = iota((1, near), 1)
    col_row = jnp.full((1, near), -1, jnp.int32)
    for r in range(rows):
        ok = (lane_near >= r * resident) & (lane_near < r * resident + len_s[r])
        col_row = jnp.where(ok, r, col_row)
    live_near = col_row == in_row % rows
    s_near = jnp.where(live_near, dot_nt(q_near, rk[...]) * scale, NEG)
    peak_near = jnp.max(s_near, axis=1, keepdims=True)
    p_near = jnp.where(live_near, jnp.exp(s_near - peak_near), 0.0)
    total_near = jnp.sum(p_near, axis=1, keepdims=True)
    sum_near = own_head(dot(p_near.astype(BF16), rv[...]), heads, in_head)

    fresh_all = pltpu.make_async_remote_copy(
        src_ref=fin.at[pl.ds(0, tps - 1)],
        dst_ref=fin.at[pl.ds(0, tps - 1)],
        send_sem=sem_f.at[0],
        recv_sem=sem_f.at[1],
        device_id=(me, z),
        device_id_type=MESH,
    )
    fresh_all.wait_recv()
    fr = rows * steps * 8
    ri, rl = iota((fr, fr), 0), iota((fr, fr), 1)
    want = (ri % rows) * (steps * 8) + (ri // rows % steps) * 8 + ri // (rows * steps)
    order = jnp.where(rl == want, 1.0, 0.0).astype(BF16)
    sorted_fresh = dot(order, fin[...].reshape(fr, fw)).astype(BF16)
    new = rows * steps
    fn = jnp.concatenate(
        [sorted_fresh[c * new : (c + 1) * new, :] for c in range(8)], axis=1
    )
    f_step = iota((new, 1), 0) // rows
    f_cos = jnp.zeros((new, HD), F32)
    f_sin = jnp.zeros((new, HD), F32)
    bc = CTX // SPAN
    for t in range(steps):
        c0, s0 = tab_v[bc : bc + 1, :], tab_v[nb + bc : nb + bc + 1, :]
        c1, s1 = tok_cos[t : t + 1, :], tok_sin[t : t + 1, :]
        f_cos = jnp.where(f_step == t, c0 * c1 - s0 * s1, f_cos)
        f_sin = jnp.where(f_step == t, s0 * c1 + c0 * s1, f_sin)
    raw = dot(fn, wk[...])
    fk = jnp.concatenate([turn(b, f_cos, f_sin) for b in per_head(raw, heads)], axis=1).astype(BF16)
    fv = dot(fn, wv[...]).astype(BF16)

    lane_new = iota((1, new), 1)
    live_new = (lane_new % rows == in_row % rows) & (lane_new // rows <= in_row // (rows * heads))
    s_new = jnp.where(live_new, dot_nt(q_near, fk) * scale, NEG)
    peak_n = jnp.maximum(peak_near, jnp.max(s_new, axis=1, keepdims=True))
    p_new = jnp.where(live_new, jnp.exp(s_new - peak_n), 0.0)
    keep = jnp.exp(peak_near - peak_n)
    total_n = keep * total_near + jnp.sum(p_new, axis=1, keepdims=True)
    o_near = keep * sum_near + own_head(dot(p_new.astype(BF16), fv), heads, in_head)

    third = iota((HD, HD), 0)
    add_up = jnp.where((third == 0) | (third == 32) | (third == 64), 1.0, 0.0).astype(BF16)
    eye = iota((inner, inner), 0) == iota((inner, inner), 1)
    peak_lane = jnp.sum(jnp.where(eye, peak_n, 0.0), axis=0, keepdims=True)
    collect_v[...] = jnp.where(pick_t, 1.0, 0.0).astype(BF16)
    add_v[...] = add_up
    from_all = pltpu.make_async_remote_copy(
        src_ref=pob.at[pl.ds(0, engines - 1)],
        dst_ref=pib.at[pl.ds(0, engines - 1)],
        send_sem=sem_p.at[0],
        recv_sem=sem_p.at[1],
        device_id=(me, z),
        device_id_type=MESH,
    )
    from_all.wait_recv()
    pin = pib[...].astype(F32)
    o_in = pin[:, :sh, :].reshape(pairs, HD)
    parts = pin[:, sh:, :].reshape(pairs, HD).astype(BF16)
    lse_in = dot(parts, add_v[...])
    top = jnp.maximum(
        jnp.max(jnp.where(pick, lse_in[:, :inner], NEG), axis=0, keepdims=True), peak_lane
    )
    top_pair = jnp.sum(jnp.where(pick, top, 0.0), axis=1, keepdims=True)
    top_in = jnp.sum(jnp.where(eye, top, 0.0), axis=1, keepdims=True)
    valid = row_col > 0.0
    w_in = jnp.where(valid, jnp.exp(jnp.where(valid, lse_in - top_pair, 0.0)), 0.0)
    weighted = jnp.concatenate(
        [jnp.where(valid, w_in * o_in, 0.0), w_in], axis=1
    )
    first = weighted.astype(BF16)
    second = (weighted - first.astype(F32)).astype(BF16)
    gathered = dot(collect_v[...], first) + dot(collect_v[...], second)
    w_near = jnp.exp(peak_n - top_in)
    result = (w_near * o_near + gathered[:, :HD]) / (w_near * total_n + gathered[:, HD:])
    for t in range(steps):
        for h in range(heads):
            j = t * heads + h
            out_v[t, :, h * HD : (h + 1) * HD] = result[j * rows : (j + 1) * rows, :].astype(BF16)

    everyone.wait_send()
    fresh_all.wait_send()
    from_all.wait_send()


def per_device(
    engines,
    tps,
    outgoing,
    span_target,
    span_row,
    span_block,
    span_tokens,
    norm_gain,
    key_weight,
    value_weight,
    fresh_states,
    queries,
    res_keys,
    res_values,
    res_len,
):
    sends, span, depth = outgoing.shape
    width = key_weight.shape[1]
    steps, rows, _ = queries.shape
    resident = res_keys.shape[1]
    heads = width // HD
    sh = steps * heads
    tokens = sends * span
    vmem = pl.BlockSpec(memory_space=pltpu.VMEM)
    hbm = pl.BlockSpec(memory_space=pltpu.HBM)
    chunks = len(chunk_bounds(depth))
    table = jnp.asarray(rope_tables(steps))
    return pl.pallas_call(
        functools.partial(kernel, engines, tps, sends, rows, steps),
        out_shape=jax.ShapeDtypeStruct((steps, rows, width), BF16),
        in_specs=[hbm] * 14,
        out_specs=vmem,
        scratch_shapes=[
            pltpu.VMEM((tokens, depth), BF16),
            pltpu.VMEM((tokens, depth), BF16),
            pltpu.VMEM((depth, width), BF16),
            pltpu.VMEM((depth, width), BF16),
            pltpu.VMEM((rows * resident, width), BF16),
            pltpu.VMEM((rows * resident, width), BF16),
            pltpu.VMEM((tokens, width), F32),
            pltpu.VMEM((tokens, width), F32),
            pltpu.VMEM((tokens, width), BF16),
            pltpu.VMEM((tokens, width), BF16),
            pltpu.VMEM((tokens, HD), F32),
            pltpu.VMEM((tokens, HD), F32),
            pltpu.VMEM((tokens, HD), F32),
            pltpu.VMEM((steps * 8, depth // 8), F32),
            pltpu.VMEM((steps * 8, depth // 8), BF16),
            pltpu.VMEM((tps, steps * 8, depth // 8), BF16),
            pltpu.VMEM((engines, sh, HD), BF16),
            pltpu.VMEM((engines, sh, HD), BF16),
            pltpu.VMEM((engines, 2 * sh, HD), BF16),
            pltpu.VMEM((engines, 2 * sh, HD), BF16),
            pltpu.VMEM((engines * sh, sends * sh), BF16),
            pltpu.VMEM((sh * rows, engines * sh), BF16),
            pltpu.VMEM((HD, HD), BF16),
            pltpu.SMEM((sends, engines), jnp.int32),
            pltpu.SMEM((sends, engines), jnp.int32),
            pltpu.SMEM((sends, engines), jnp.int32),
            pltpu.SMEM((rows,), jnp.int32),
            pltpu.VMEM((sends, engines), jnp.int32),
            pltpu.VMEM((sends, engines), jnp.int32),
            pltpu.VMEM((depth // HD, HD), F32),
            pltpu.VMEM(table.shape, F32),
            pltpu.VMEM((steps, depth), BF16),
            pltpu.VMEM((steps, rows, width), BF16),
            pltpu.SemaphoreType.DMA((chunks,)),
            pltpu.SemaphoreType.DMA((2, chunks)),
            pltpu.SemaphoreType.DMA((2,)),
            pltpu.SemaphoreType.DMA((10,)),
            pltpu.SemaphoreType.REGULAR,
            pltpu.SemaphoreType.DMA((2,)),
            pltpu.SemaphoreType.DMA((2,)),
            pltpu.SemaphoreType.DMA((2,)),
        ],
        compiler_params=pltpu.CompilerParams(
            collective_id=0, has_side_effects=True, vmem_limit_bytes=60 * 1024 * 1024
        ),
    )(
        outgoing.reshape(tokens, depth),
        span_target.T,
        span_row.T,
        span_block.T,
        span_tokens.T,
        res_len,
        norm_gain.reshape(depth // HD, HD),
        table,
        fresh_states.reshape(steps, depth),
        queries,
        key_weight,
        value_weight,
        res_keys.reshape(rows * resident, width),
        res_values.reshape(rows * resident, width),
    )


def solution(mesh):
    in_specs = (
        P("engine", None, None),
        P(),
        P(),
        P(),
        P(),
        P(),
        P(None, "tp"),
        P(None, "tp"),
        P(None, ("engine", "tp"), None),
        P(None, "engine", "tp"),
        P("engine", None, "tp"),
        P("engine", None, "tp"),
        P("engine"),
    )
    return jax.shard_map(
        functools.partial(per_device, mesh.shape["engine"], mesh.shape["tp"]),
        mesh=mesh,
        in_specs=in_specs,
        out_specs=P(None, "engine", "tp"),
        check_vma=False,
    )
```
